128 devices in a mesh: fsdp: 4 (over y), ctx: 32 (over z, x, core).
Axes of the slice: x: 4, y: 4, z: 4, core: 2. Of those that a mesh axis runs over, the one named last changes fastest.
Arguments:
- tokens: bfloat16 [16384, 640], P(('fsdp', 'ctx')), may hold values from -6 to 6
- positions: int32 [16384], P(('fsdp', 'ctx')), may hold values from 0 to 12285, as said below
- w_query: bfloat16 [640, 1024], P('fsdp'), may hold values from -0.25 to 0.25
- w_key: bfloat16 [640, 256], P('fsdp'), may hold values from -0.25 to 0.25
- w_value: bfloat16 [640, 256], P('fsdp'), may hold values from -0.25 to 0.25
- w_out: bfloat16 [1024, 640], P('fsdp'), may hold values from -0.1875 to 0.1875
- w_gate: bfloat16 [640, 2048], P('fsdp'), may hold values from -0.25 to 0.25
- w_up: bfloat16 [640, 2048], P('fsdp'), may hold values from -0.25 to 0.25
- w_down: bfloat16 [2048, 640], P('fsdp'), may hold values from -0.125 to 0.125
- gain_in: bfloat16 [640], P('fsdp'), may hold values from 0.5 to 1.5
- gain_query: bfloat16 [256], P('fsdp'), may hold values from 0.099609375 to 1.8984375
- gain_key: bfloat16 [256], P('fsdp'), may hold values from 0.099609375 to 1.8984375
- gain_attn_post: bfloat16 [640], P('fsdp'), may hold values from 0.5 to 1.5
- gain_ffn_pre: bfloat16 [640], P('fsdp'), may hold values from 0.5 to 1.5
- gain_ffn_post: bfloat16 [640], P('fsdp'), may hold values from 0.5 to 1.5
- cotangent: bfloat16 [16384, 640], P(('fsdp', 'ctx')), may hold values from -6 to 6
Outputs:
- layer_out: bfloat16 [16384, 640], P(('fsdp', 'ctx'))
- input_grad: float32 [16384, 640], P(('fsdp', 'ctx'))
- w_query_grad: float32 [640, 1024], P('fsdp')
- w_key_grad: float32 [640, 256], P('fsdp')
- w_value_grad: float32 [640, 256], P('fsdp')
- w_out_grad: float32 [1024, 640], P('fsdp')
- w_gate_grad: float32 [640, 2048], P('fsdp')
- w_up_grad: float32 [640, 2048], P('fsdp')
- w_down_grad: float32 [2048, 640], P('fsdp')
- gain_in_grad: float32 [640], P('fsdp')
- gain_query_grad: float32 [256], P('fsdp')
- gain_key_grad: float32 [256], P('fsdp')
- gain_attn_post_grad: float32 [640], P('fsdp')
- gain_ffn_pre_grad: float32 [640], P('fsdp')
- gain_ffn_post_grad: float32 [640], P('fsdp')
The draws below stay inside these ranges and needn't reach their ends.
Inputs may be any that keep to these rules, and one draw needn't show every extreme that they name: `positions`: within each sequence of 4096 tokens the ids start at 0 and rise by 1 to 3 from one token to the next; in one sequence they rise by 3 at every token.
All inputs are finite; a program needn't handle non-finite values.
Results may differ from the reference program's by a relative error of at most 0.033.
Values may be sent and summed in bfloat16 or wider, within the bound.
A program may use at most 128 MiB of HBM per device.

```python
import jax
import jax.numpy as jnp
from jax import lax

D = 640
H = 4
HD = 256
FF = 2048
QD = 1024
SEQ_LEN = 4096
TOKENS = 16384


def draw_positions(key, part):
    key = jax.random.fold_in(key, 7)
    seq_count = TOKENS // SEQ_LEN
    step_key, pick_key = jax.random.split(key)
    increments = jax.random.randint(step_key, (seq_count, SEQ_LEN), 1, 4, dtype=jnp.int32)
    chosen = jax.random.randint(pick_key, (), 0, seq_count, dtype=jnp.int32)
    row_ids = jnp.arange(seq_count, dtype=jnp.int32)[:, None]
    increments = jnp.where(row_ids == chosen, jnp.full_like(increments, 3), increments)
    first_column = jnp.arange(SEQ_LEN, dtype=jnp.int32)[None, :] == 0
    increments = jnp.where(first_column, jnp.zeros_like(increments), increments)
    return jnp.cumsum(increments, axis=1).reshape(seq_count * SEQ_LEN).astype(jnp.int32)


def steps_of(key, shape, cuts, smallest, high):
    def one(position, parts):
        draws = jax.random.uniform(jax.random.fold_in(jax.random.fold_in(key, 6), position), (parts,), jnp.float32, smallest / len(cuts), high / len(cuts))
        return jnp.repeat(jnp.exp(draws), shape[position] // parts).reshape((-1,) + (1,) * (len(shape) - position - 1))

    gain = one(*cuts[0])
    for cut in cuts[1:]:
        gain = gain * one(*cut)
    return gain


def bell_draw(rng, extent, deviation, limit, shards=(), held_as=jnp.bfloat16):
    level = steps_of(rng, extent, shards, -0.22, 0.18) if shards else 1.0
    values = jax.random.normal(rng, extent, jnp.float32) * deviation * level
    return jnp.minimum(jnp.maximum(values, -limit), limit).astype(held_as)


def setup_inputs(seed: int = 0) -> dict:
    keys = jax.random.split(jax.random.key(seed), 17)
    return {
        "tokens": bell_draw(keys[0], (TOKENS, D), 1.0, 6.0, ((0, 128),)),
        "positions": draw_positions(jax.random.fold_in(keys[16], 71), 0),
        "w_query": bell_draw(keys[2], (D, QD), D ** -0.5, 0.25, ((0, 4),)),
        "w_key": bell_draw(keys[3], (D, HD), D ** -0.5, 0.25, ((0, 4),)),
        "w_value": bell_draw(keys[4], (D, HD), D ** -0.5, 0.25, ((0, 4),)),
        "w_out": bell_draw(keys[5], (QD, D), QD ** -0.5, 0.1875, ((0, 4),)),
        "w_gate": bell_draw(keys[6], (D, FF), D ** -0.5, 0.25, ((0, 4),)),
        "w_up": bell_draw(keys[7], (D, FF), D ** -0.5, 0.25, ((0, 4),)),
        "w_down": bell_draw(keys[8], (FF, D), FF ** -0.5, 0.125, ((0, 4),)),
        "gain_in": jnp.clip(1.0 + 0.1 * jax.random.normal(keys[9], (D,), jnp.float32), 0.5, 1.5).astype(jnp.bfloat16),
        "gain_query": jnp.clip(1.0 + 0.18 * jax.random.normal(keys[10], (HD,), jnp.float32), 0.099609375, 1.8984375).astype(jnp.bfloat16),
        "gain_key": jnp.clip(1.0 + 0.18 * jax.random.normal(keys[11], (HD,), jnp.float32), 0.099609375, 1.8984375).astype(jnp.bfloat16),
        "gain_attn_post": jnp.clip(1.0 + 0.1 * jax.random.normal(keys[12], (D,), jnp.float32), 0.5, 1.5).astype(jnp.bfloat16),
        "gain_ffn_pre": jnp.clip(1.0 + 0.1 * jax.random.normal(keys[13], (D,), jnp.float32), 0.5, 1.5).astype(jnp.bfloat16),
        "gain_ffn_post": jnp.clip(1.0 + 0.1 * jax.random.normal(keys[14], (D,), jnp.float32), 0.5, 1.5).astype(jnp.bfloat16),
        "cotangent": bell_draw(keys[15], (TOKENS, D), 1.0, 6.0, ((0, 128),)),
    }


EPSILON = 1e-06
ROPE_BASE = 1000000.0
SCORE_SCALE = 0.0625
MASK_VALUE = -1e+30
HIGHEST = lax.Precision.HIGHEST

@jax.custom_vjp
def low(v):
    return lax.optimization_barrier(v.astype(jnp.bfloat16)).astype(jnp.float32)

@jax.custom_vjp
def low_back(v):
    return v

def low_keep(v):
    return (low(v), None)

def low_pass(kept, grad):
    return (grad,)

def back_keep(v):
    return (v, None)

def back_low(kept, grad):
    return (low(grad),)
low.defvjp(low_keep, low_pass)
low_back.defvjp(back_keep, back_low)

def product(left_side, right_side):
    return jnp.dot(left_side, right_side, precision=HIGHEST, preferred_element_type=jnp.float32)

def rms_scale(values, gain_vector):
    return values * lax.rsqrt(lax.optimization_barrier(jnp.mean(values * values, axis=-1, keepdims=True)) + EPSILON) * gain_vector

def rotate(values, cosine, sine_table):
    half_size = values.shape[-1] // 2
    first_half = values[..., :half_size]
    second_half = values[..., half_size:]
    return jnp.concatenate([first_half * cosine - second_half * sine_table, second_half * cosine + first_half * sine_table], axis=-1)

def rope_tables(positions, head_dim):
    exponents = jnp.arange(0, head_dim, 2, dtype=jnp.float32) / head_dim
    inverse = 1.0 / ROPE_BASE ** exponents
    angles = positions.astype(jnp.float32)[:, None] * inverse[None, :]
    return (jnp.cos(angles), jnp.sin(angles))

def block_forward(inputs, positions, query_w, key_w, value_w, out_w, gate_w, up_w, down_w, gain_in, gain_query, gain_key, gain_attn, gain_pre, gain_post):
    seq_len = inputs.shape[0]
    normed = low(rms_scale(inputs, gain_in))
    query_raw = low_back(product(normed, query_w))
    key_raw = low_back(product(normed, key_w))
    value_low = low_back(low(product(normed, value_w)))
    cosine, sine_table = rope_tables(positions, HD)
    query_heads = rms_scale(query_raw.reshape(seq_len, H, HD), gain_query)
    query_rows = low(rotate(query_heads, cosine[:, None, :], sine_table[:, None, :])).reshape(seq_len * H, HD)
    key_low = low(rotate(rms_scale(key_raw, gain_key), cosine, sine_table))
    block_tok = min(512, seq_len)
    key_pos = jnp.arange(seq_len, dtype=jnp.int32)

    def attend(block_pair):
        query_block, first_tok = block_pair
        row_pos = first_tok + jnp.arange(block_tok * H, dtype=jnp.int32) // H
        scores = low_back(product(query_block, key_low.T) * SCORE_SCALE)
        scores = jnp.where(key_pos[None, :] <= row_pos[:, None], scores, MASK_VALUE)
        probs = low(jax.nn.softmax(scores, axis=-1))
        return product(probs, value_low)
    blocks = query_rows.reshape(seq_len // block_tok, block_tok * H, HD)
    starts = jnp.arange(seq_len // block_tok, dtype=jnp.int32) * block_tok
    attended = lax.map(jax.checkpoint(attend), (blocks, starts))
    attn_out = low_back(low(attended.reshape(seq_len, H * HD)))
    proj = low_back(product(attn_out, out_w))
    hidden = inputs + rms_scale(proj, gain_attn)
    ffn_in = low(rms_scale(hidden, gain_pre))
    gate_value = low_back(product(ffn_in, gate_w))
    up_value = low_back(product(ffn_in, up_w))
    mixed = low(jax.nn.gelu(gate_value, approximate=True) * up_value)
    down_value = low_back(product(mixed, down_w))
    return hidden + rms_scale(down_value, gain_post)

def reference(tokens, positions, w_query, w_key, w_value, w_out, w_gate, w_up, w_down, gain_in, gain_query, gain_key, gain_attn_post, gain_ffn_pre, gain_ffn_post, cotangent):
    params = tuple((weight_array.astype(jnp.float32) for weight_array in (w_query, w_key, w_value, w_out, w_gate, w_up, w_down, gain_in, gain_query, gain_key, gain_attn_post, gain_ffn_pre, gain_ffn_post)))
    seq_count = TOKENS // SEQ_LEN
    seq_tokens = tokens.astype(jnp.float32).reshape(seq_count, SEQ_LEN, D)
    seq_pos = positions.reshape(seq_count, SEQ_LEN)
    seq_cot = cotangent.astype(jnp.float32).reshape(seq_count, SEQ_LEN, D)

    def one_sequence(totals, seq_items):
        inputs, pos_seq, cot_seq = seq_items

        def forward(inputs_f, *weights):
            return block_forward(inputs_f, pos_seq, *weights)
        output, pullback = jax.vjp(forward, inputs, *params)
        gradients = pullback(cot_seq)
        new_totals = tuple((total + grad_item for total, grad_item in zip(totals, gradients[1:])))
        return (new_totals, (output.astype(jnp.bfloat16), gradients[0]))
    start_totals = tuple((jnp.zeros_like(param_item) for param_item in params))
    totals, (outputs, input_grads) = lax.scan(one_sequence, start_totals, (seq_tokens, seq_pos, seq_cot))
    return (outputs.reshape(TOKENS, D), input_grads.reshape(TOKENS, D), totals[0], totals[1], totals[2], totals[3], totals[4], totals[5], totals[6], totals[7], totals[8], totals[9], totals[10], totals[11], totals[12])
```

```python
import functools

import jax
import jax.numpy as jnp
from jax import lax
from jax.experimental import pallas as pl
from jax.experimental.pallas import tpu as pltpu
from jax.sharding import PartitionSpec as P

EPS = 1e-06
ROPE_BASE = 1000000.0
BF = jnp.bfloat16
F32 = jnp.float32
MESH = pl.DeviceIdType.MESH
VMEM = pltpu.VMEM
VSPEC = pl.BlockSpec(memory_space=pltpu.VMEM)
ANYSPEC = pl.BlockSpec(memory_space=pl.ANY)
VMEM_LIMIT = 60 * 1024 * 1024
C_ROOT = 0.7978845608028654
C_CUBE = 0.044715

PART_UNITS = (96, 128, 128)
PART_OFF = (0, 1536, 3584)
ROWS = 5632
OFF_Q, OFF_K, OFF_V, OFF_G, OFF_U, OFF_O, OFF_D, OFF_GAIN = 0, 640, 800, 960, 2240, 3520, 4160, 5440
GAIN_ROWS = 16


class Net:
    def __init__(self, send_sem, recv_sem):
        me = lax.axis_index("ctx")
        self.y = lax.axis_index("fsdp")
        self.c = lax.rem(me, 2)
        self.x = lax.rem(lax.div(me, 2), 4)
        self.z = lax.div(me, 8)
        self.send_sem, self.recv_sem = send_sem, recv_sem
        self.used = 0
        self.sent = []

    def pos(self, axis):
        return {"x": self.x, "y": self.y, "z": self.z, "c": self.c}[axis]

    def at(self, axis, step):
        return lax.rem(self.pos(axis) + (step + 4), 4)

    def dev(self, axis, step):
        x, y, z, c = self.x, self.y, self.z, self.c
        if axis == "x":
            x = self.at("x", step)
        elif axis == "y":
            y = self.at("y", step)
        elif axis == "z":
            z = self.at("z", step)
        else:
            c = 1 - c
        return {"fsdp": y, "ctx": z * 8 + x * 2 + c}

    def copy(self, src, dst, axis, step=1):
        k = self.used
        self.used += 1
        cp = pltpu.make_async_remote_copy(
            src_ref=src,
            dst_ref=dst,
            send_sem=self.send_sem.at[k],
            recv_sem=self.recv_sem.at[k],
            device_id=self.dev(axis, step),
            device_id_type=MESH,
        )
        cp.start()
        self.sent.append(cp)
        return cp

    def barrier(self, peers):
        sem = pltpu.get_barrier_semaphore()
        for axis, step in peers:
            pl.semaphore_signal(sem, inc=1, device_id=self.dev(axis, step), device_id_type=MESH)
        pl.semaphore_wait(sem, len(peers))

    def drain(self):
        for cp in self.sent:
            cp.wait_send()


class Gather:
    def __init__(self, net, axis, piece):
        self.net, self.axis, self.piece = net, axis, piece

    def start(self):
        own = self.piece(self.net.pos(self.axis), None)
        self.up = self.net.copy(own, own, self.axis, 1)
        self.down = self.net.copy(own, own, self.axis, -1)

    def mid(self):
        self.up.wait_recv()
        low = self.piece(self.net.at(self.axis, -1), 0)
        self.up2 = self.net.copy(low, low, self.axis, 1)
        self.down.wait_recv()
        high = self.piece(self.net.at(self.axis, 1), 1)
        self.down2 = self.net.copy(high, high, self.axis, -1)

    def end(self):
        self.up2.wait_recv()
        self.down2.wait_recv()


class Scatter:
    def __init__(self, net, axis, q, bufs, add):
        self.net, self.axis, self.q, self.bufs, self.add = net, axis, q, bufs, add

    def start(self):
        lo, hi, _, _ = self.bufs
        far = self.net.at(self.axis, 2)
        self.cl = self.net.copy(self.q(far, 0), lo, self.axis, 1)
        self.ch = self.net.copy(self.q(far, 1), hi, self.axis, -1)

    def mid(self):
        lo, hi, rp, rm = self.bufs
        up, down = self.net.at(self.axis, 1), self.net.at(self.axis, -1)
        self.cl.wait_recv()
        self.add(self.q(up, 0), (lo,))
        self.cp = self.net.copy(self.q(up, None), rp, self.axis, 1)
        self.ch.wait_recv()
        self.add(self.q(down, 1), (hi,))
        self.cm = self.net.copy(self.q(down, None), rm, self.axis, -1)

    def end(self, out=None):
        _, _, rp, rm = self.bufs
        self.cp.wait_recv()
        self.cm.wait_recv()
        self.add(self.q(self.net.pos(self.axis), None), (rp, rm), out)


def add_rows(dst, srcs, out=None, out_dtype=BF):
    target = dst if out is None else out
    lead, rows = dst.shape[:-2], dst.shape[-2]
    step = 32 if rows % 32 == 0 else 16
    count = 1
    for n in lead:
        count *= n
    per = rows // step

    def body(i, _):
        r = pl.ds(pl.multiple_of(lax.rem(i, per) * step, 16), step)
        k = lax.div(i, per)
        idx = []
        for n in reversed(lead):
            idx.insert(0, lax.rem(k, n))
            k = lax.div(k, n)
        idx = (*idx, r, slice(None))
        total = dst[idx].astype(F32)
        for s in srcs:
            total += s[idx].astype(F32)
        target[idx] = total.astype(target.dtype)
        return 0

    lax.fori_loop(0, count * per, body, 0)


def weights_kernel(
    wq, wk, wv, wo, wg, wu, wd, gains, qkv_all, gu_all, wo_all, wd_all, gain_all, send_sem, recv_sem, own_sem
):
    net = Net(send_sem, recv_sem)
    y, c, x, z = net.y, net.c, net.x, net.z
    own = [
        (wq, qkv_all.at[y, :, pl.ds(0, 1024)]),
        (wk, qkv_all.at[y, :, pl.ds(1024, 256)]),
        (wv, qkv_all.at[y, :, pl.ds(1280, 256)]),
        (wo, wo_all.at[y]),
        (wg, gu_all.at[y, :, pl.ds(0, 2048)]),
        (wu, gu_all.at[y, :, pl.ds(2048, 2048)]),
        (wd, wd_all.at[y]),
        (gains, gain_all.at[y]),
    ]
    copies = []
    for k, (src, dst) in enumerate(own):
        cp = pltpu.make_async_copy(src, dst, own_sem.at[k])
        cp.start()
        copies.append(cp)
    net.barrier([("c", 1), ("x", 1), ("x", -1), ("y", 1), ("y", -1), ("y", 2), ("z", 1), ("z", -1)])
    for cp in copies:
        cp.wait()
    rows = pl.ds(pl.multiple_of(c * 80, 16), 80)

    def qkv_piece(yq, a, half):
        off, n = {None: (0, 384), 0: (0, 128), 1: (128, 256)}[half]
        return qkv_all.at[yq, rows, pl.ds(pl.multiple_of(a * 384 + off, 128), n)]

    def gu_piece(yq, a, half):
        off, n = {None: (0, 1024), 0: (0, 512), 1: (512, 512)}[half]
        return gu_all.at[yq, rows, pl.ds(pl.multiple_of(a * 1024 + off, 128), n)]

    def wo_piece(yq, a, half):
        off, n = {None: (0, 32), 0: (0, 16), 1: (16, 16)}[half]
        return wo_all.at[yq, pl.ds(pl.multiple_of(c * 128 + a * 32 + off, 16), n)]

    def wd_piece(yq, a, half):
        off, n = {None: (0, 64), 0: (0, 32), 1: (32, 32)}[half]
        return wd_all.at[yq, pl.ds(pl.multiple_of(c * 256 + a * 64 + off, 16), n)]

    def swap_of(k, yq):
        return (
            lambda: qkv_all.at[yq, rows],
            lambda: gu_all.at[yq, rows],
            lambda: wo_all.at[yq, pl.ds(pl.multiple_of(c * 128, 16), 128)],
            lambda: wd_all.at[yq, pl.ds(pl.multiple_of(c * 256, 16), 256)],
        )[k]()

    pieces = (qkv_piece, gu_piece, wo_piece, wd_piece)
    axes = ("z", "x", "z", "z")
    gain_own = gain_all.at[y]
    gain_copies = [net.copy(gain_own, gain_own, "y", s) for s in (1, -1, 2)]
    along_y = []
    for piece, axis in zip(pieces, axes):
        g = Gather(net, "y", functools.partial(lambda piece, a, yq, half: piece(yq, a, half), piece, net.pos(axis)))
        g.start()
        along_y.append(g)
    planes = {}

    def plane(k, step):
        yq = net.at("y", step)
        g = Gather(net, axes[k], functools.partial(pieces[k], yq))
        g.start()
        planes[k, step] = g

    for k in range(4):
        along_y[k].mid()
        plane(k, -1)
        plane(k, 1)
    for k in range(4):
        along_y[k].end()
        plane(k, 2)
    swaps = []
    for step in (-1, 1, 2):
        for k in range(4):
            planes[k, step].mid()
    for step in (-1, 1, 2):
        for k in range(4):
            planes[k, step].end()
            ref = swap_of(k, net.at("y", step))
            swaps.append(net.copy(ref, ref, "c"))
    for cp in (*swaps, *gain_copies):
        cp.wait_recv()
    net.drain()


def gather_weights(wq, wk, wv, wo, wg, wu, wd, gains):
    n = 3 + 16 + 48 + 12
    return pl.pallas_call(
        weights_kernel,
        out_shape=(
            jax.ShapeDtypeStruct((4, 160, 1536), BF),
            jax.ShapeDtypeStruct((4, 160, 4096), BF),
            jax.ShapeDtypeStruct((4, 256, 640), BF),
            jax.ShapeDtypeStruct((4, 512, 640), BF),
            jax.ShapeDtypeStruct((4, 16, 128), BF),
        ),
        in_specs=[ANYSPEC] * 8,
        out_specs=[ANYSPEC] * 5,
        scratch_shapes=[
            pltpu.SemaphoreType.DMA((n,)),
            pltpu.SemaphoreType.DMA((n,)),
            pltpu.SemaphoreType.DMA((8,)),
        ],
        compiler_params=pltpu.CompilerParams(collective_id=0, has_side_effects=True, vmem_limit_bytes=VMEM_LIMIT),
        name="gather_weights",
    )(wq, wk, wv, wo, wg, wu, wd, gains)


def half_rows(half):
    return {None: slice(None), 0: pl.ds(0, 64), 1: pl.ds(64, 64)}[half]


def keys_kernel(k, v, k_all, v_all, send_sem, recv_sem, own_sem):
    net = Net(send_sem, recv_sem)
    c, x, z = net.c, net.x, net.z
    own = [pltpu.make_async_copy(k, k_all.at[c, z, x], own_sem.at[0]), pltpu.make_async_copy(v, v_all.at[c, z, x], own_sem.at[1])]
    for cp in own:
        cp.start()
    net.barrier([("c", 1), ("x", 1), ("x", -1), ("z", 1), ("z", -1)])
    for cp in own:
        cp.wait()
    kx = Gather(net, "x", lambda j, h: k_all.at[c, z, j, half_rows(h)])
    vz = Gather(net, "z", lambda j, h: v_all.at[c, j, x, half_rows(h)])
    kz = Gather(net, "z", lambda j, h: k_all.at[c, j, :, half_rows(h)])
    vx = Gather(net, "x", lambda j, h: v_all.at[c, :, j, half_rows(h)])
    for g in (kx, vz):
        g.start()
    for g in (kx, vz):
        g.mid()
    for g in (kx, vz):
        g.end()
    kz.start()
    vx.start()
    swaps = []

    def swap_k(j):
        ref = k_all.at[c, j]
        swaps.append(net.copy(ref, ref, "c"))

    def swap_v(j):
        ref = v_all.at[c, :, j]
        swaps.append(net.copy(ref, ref, "c"))

    swap_k(z)
    swap_v(x)
    kz.mid()
    vx.mid()
    for s in (-1, 1):
        swap_k(net.at("z", s))
        swap_v(net.at("x", s))
    kz.end()
    vx.end()
    swap_k(net.at("z", 2))
    swap_v(net.at("x", 2))
    for cp in swaps:
        cp.wait_recv()
    net.drain()


def gather_keys(k, v):
    n = 16 + 8
    shape = jax.ShapeDtypeStruct((2, 4, 4, 128, 256), BF)
    return pl.pallas_call(
        keys_kernel,
        out_shape=(shape, shape),
        in_specs=[ANYSPEC] * 2,
        out_specs=[ANYSPEC] * 2,
        scratch_shapes=[
            pltpu.SemaphoreType.DMA((n,)),
            pltpu.SemaphoreType.DMA((n,)),
            pltpu.SemaphoreType.DMA((2,)),
        ],
        compiler_params=pltpu.CompilerParams(collective_id=1, has_side_effects=True, vmem_limit_bytes=VMEM_LIMIT),
        name="gather_keys",
    )(k, v)


def key_grads_kernel(
    dk, dv, dk_out, dv_out, kin, vin, k1lo, k1hi, k1p, k1m, v1lo, v1hi, v1p, v1m,
    k2lo, k2hi, k2p, k2m, v2lo, v2hi, v2p, v2m, send_sem, recv_sem,
):
    net = Net(send_sem, recv_sem)
    c, x, z = net.c, net.x, net.z
    net.barrier([("c", 1), ("x", 1), ("x", -1), ("z", 1), ("z", -1)])
    other = 1 - c
    kc, vc = {}, {}
    for s in (2, 1, -1, 0):
        j = net.at("z", s)
        kc[s] = net.copy(dk.at[other, j], kin.at[j], "c")
        j = net.at("x", s)
        vc[s] = net.copy(dv.at[other, :, j], vin.at[:, j], "c")

    def take(s):
        j = net.at("z", s)
        kc[s].wait_recv()
        add_rows(kin.at[j], (dk.at[c, j],))
        j = net.at("x", s)
        vc[s].wait_recv()
        add_rows(vin.at[:, j], (dv.at[c, :, j],))

    k1 = Scatter(net, "z", lambda j, h: kin.at[j, :, half_rows(h)], (k1lo, k1hi, k1p, k1m), add_rows)
    v1 = Scatter(net, "x", lambda j, h: vin.at[:, j, half_rows(h)], (v1lo, v1hi, v1p, v1m), add_rows)
    k2 = Scatter(net, "x", lambda j, h: kin.at[z, j, half_rows(h)], (k2lo, k2hi, k2p, k2m), add_rows)
    v2 = Scatter(net, "z", lambda j, h: vin.at[j, x, half_rows(h)], (v2lo, v2hi, v2p, v2m), add_rows)
    take(2)
    k1.start()
    v1.start()
    take(1)
    take(-1)
    k1.mid()
    v1.mid()
    take(0)
    k1.end()
    k2.start()
    v1.end()
    v2.start()
    k2.mid()
    v2.mid()
    k2.end(dk_out)
    v2.end(dv_out)
    net.drain()


def reduce_key_grads(dk, dv):
    n = 8 + 16
    one = jax.ShapeDtypeStruct((128, 256), F32)
    big, half_big = VMEM((4, 128, 256), BF), VMEM((4, 64, 256), BF)
    small, half_small = VMEM((128, 256), BF), VMEM((64, 256), BF)
    return pl.pallas_call(
        key_grads_kernel,
        out_shape=(one, one),
        in_specs=[VSPEC] * 2,
        out_specs=[VSPEC] * 2,
        scratch_shapes=[
            VMEM((4, 4, 128, 256), BF),
            VMEM((4, 4, 128, 256), BF),
            half_big, half_big, big, big,
            half_big, half_big, big, big,
            half_small, half_small, small, small,
            half_small, half_small, small, small,
            pltpu.SemaphoreType.DMA((n,)),
            pltpu.SemaphoreType.DMA((n,)),
        ],
        compiler_params=pltpu.CompilerParams(collective_id=2, has_side_effects=True, vmem_limit_bytes=VMEM_LIMIT),
        name="reduce_key_grads",
    )(dk, dv)


def tdot(a, b):
    return lax.dot_general(a, b, (((0,), (0,)), ((), ())), preferred_element_type=F32)


def dot(a, b):
    return jnp.dot(a, b, preferred_element_type=F32)


def dot_back(a, b):
    return lax.dot_general(a, b, (((1,), (1,)), ((), ())), preferred_element_type=F32)


PART_ORDER = (("y", "z", "x"), ("x", "y", "z"), ("z", "x", "y"))
PART_MAJOR = (("z", "x"), ("x", "z"), ("z", "x"))


def scatter_shapes(part):
    u = PART_UNITS[part]
    shapes, lead, rows = [], 4, 16 * u
    for axis in PART_ORDER[part]:
        if axis == "y":
            lead = 1
        else:
            rows //= 4
        shapes.append((lead, rows))
    return shapes


def weight_grads_kernel(*refs):
    acts, gains = refs[:8], refs[8]
    full = refs[9]
    g = refs[10]
    both = refs[11:19]
    gain_in = refs[19]
    bufs = refs[20:56]
    send_sem, recv_sem, own_sem = refs[56:]
    net = Net(send_sem, recv_sem)
    y, c, x, z = net.y, net.c, net.x, net.z
    local = []
    for k in range(8):
        cp = pltpu.make_async_copy(acts[k], both[k].at[pl.ds(0, 128)], own_sem.at[k])
        cp.start()
        local.append(cp)
    net.barrier([("c", 1), ("x", 1), ("x", -1), ("y", 1), ("y", -1), ("z", 1), ("z", -1)])
    pair = [net.copy(acts[k], both[k].at[pl.ds(128, 128)], "c") for k in range(8)]
    gain_pair = net.copy(gains, gain_in, "c")
    for k in range(8):
        local[k].wait()
        pair[k].wait_recv()
    gain_pair.wait_recv()
    normed, qkvg, attn, projg, ffn, gug, mixed, downg = both

    def put(off, n, value, col_blocks):
        value = value.astype(BF)
        for yq in range(4):
            for j in range(col_blocks):
                g[yq, pl.ds(off + j * n, n), :] = value[yq * n : yq * n + n, j * 128 : j * 128 + 128]

    def cols(start, width):
        return pl.ds(pl.multiple_of(start, 128), width)

    put(OFF_Q, 160, tdot(normed[...], qkvg[:, cols(c * 512, 512)]), 4)
    put(OFF_K, 160, tdot(normed[...], qkvg[:, cols(1024 + c * 128, 128)]), 1)
    put(OFF_V, 160, tdot(normed[...], qkvg[:, cols(1280 + c * 128, 128)]), 1)
    for part in range(2):
        put(OFF_G + part * 640, 160, tdot(ffn[...], gug[:, cols(c * 1024 + part * 512, 512)]), 4)
        put(OFF_U + part * 640, 160, tdot(ffn[...], gug[:, cols(2048 + c * 1024 + part * 512, 512)]), 4)
    for yq in range(4):
        value = tdot(attn[:, cols(yq * 256 + c * 128, 128)], projg[...]).astype(BF)
        for j in range(5):
            g[yq, pl.ds(OFF_O + j * 128, 128), :] = value[:, j * 128 : j * 128 + 128]
        value = tdot(mixed[:, cols(yq * 512 + c * 256, 256)], downg[...]).astype(BF)
        for j in range(5):
            g[yq, pl.ds(OFF_D + j * 256, 256), :] = value[:, j * 128 : j * 128 + 128]
    g[:, pl.ds(OFF_GAIN, 16), :] = (gains[...] + gain_in[...]).astype(BF)
    g[:, pl.ds(OFF_GAIN + 16, ROWS - OFF_GAIN - 16), :] = jnp.zeros((4, ROWS - OFF_GAIN - 16, 128), BF)

    place = [[0, 4, PART_OFF[p], 16 * PART_UNITS[p]] for p in range(3)]

    def share(p, axis):
        y0, yn, r0, rn = place[p]

        def q(j, half):
            if axis == "y":
                ys, yc, rs, rc = j, 1, r0, rn
            else:
                ys, yc, rs, rc = y0, yn, r0 + j * (rn // 4), rn // 4
            if half is not None:
                rc //= 2
                rs = rs + half * rc
            return g.at[pl.ds(ys, yc), pl.ds(pl.multiple_of(rs, 16), rc)]

        return q

    def narrow(p, axis):
        y0, yn, r0, rn = place[p]
        if axis == "y":
            place[p] = [y, 1, r0, rn]
        else:
            place[p] = [y0, yn, r0 + net.pos(axis) * (rn // 4), rn // 4]

    for phase in range(3):
        runs = []
        for p in range(3):
            axis = PART_ORDER[p][phase]
            k = (p * 3 + phase) * 4
            runs.append(Scatter(net, axis, share(p, axis), bufs[k : k + 4], add_rows))
            runs[-1].start()
        for r in runs:
            r.mid()
        for p, r in enumerate(runs):
            narrow(p, PART_ORDER[p][phase])
            if phase < 2:
                r.end()
            else:
                _, _, r0, rn = place[p]
                r.end(full.at[pl.ds(c, 1), pl.ds(pl.multiple_of(r0, 16), rn)])

    stages = [[], []]
    for p in range(3):
        u, off = PART_UNITS[p], PART_OFF[p]
        major, minor = PART_MAJOR[p]

        def first(j, half, u=u, off=off, major=major):
            n = u if half is None else u // 2
            return full.at[c, pl.ds(pl.multiple_of(off + net.pos(major) * 4 * u + j * u + (half or 0) * n, 16), n)]

        def second(j, half, u=u, off=off):
            n = 4 * u if half is None else 2 * u
            return full.at[c, pl.ds(pl.multiple_of(off + j * 4 * u + (half or 0) * n, 16), n)]

        stages[0].append(Gather(net, minor, first))
        stages[1].append(Gather(net, major, second))
    for r in stages[0]:
        r.start()
    for r in stages[0]:
        r.mid()
    for a, b in zip(*stages):
        a.end()
        b.start()
    for r in stages[1]:
        r.mid()
    swaps = []
    for p, r in enumerate(stages[1]):
        r.end()
        ref = full.at[c, pl.ds(PART_OFF[p], 16 * PART_UNITS[p])]
        swaps.append(net.copy(ref, ref, "c"))
    for cp in swaps:
        cp.wait_recv()
    net.drain()


def reduce_weight_grads(acts, gains):
    n = 9 + 36 + 24 + 3
    bufs = []
    for p in range(3):
        for lead, rows in scatter_shapes(p):
            bufs += [VMEM((lead, rows // 2, 128), BF)] * 2 + [VMEM((lead, rows, 128), BF)] * 2
    return pl.pallas_call(
        weight_grads_kernel,
        out_shape=jax.ShapeDtypeStruct((2, ROWS, 128), BF),
        in_specs=[VSPEC] * 9,
        out_specs=VSPEC,
        scratch_shapes=[
            VMEM((4, ROWS, 128), BF),
            *[VMEM((256, a.shape[1]), BF) for a in acts],
            VMEM((4, 16, 128), F32),
            *bufs,
            pltpu.SemaphoreType.DMA((n,)),
            pltpu.SemaphoreType.DMA((n,)),
            pltpu.SemaphoreType.DMA((8,)),
        ],
        compiler_params=pltpu.CompilerParams(collective_id=3, has_side_effects=True, vmem_limit_bytes=VMEM_LIMIT),
        name="reduce_weight_grads",
    )(*acts, gains)


def unpack_kernel(full, oq, ok, ov, oo, og, ou, od, ogain):
    for c in range(2):
        def block(off, n, j):
            return full[c, pl.ds(off + j * n, n), :].astype(F32)

        for j in range(4):
            oq[:, pl.ds(c * 512 + j * 128, 128)] = block(OFF_Q, 160, j)
        ok[:, pl.ds(c * 128, 128)] = block(OFF_K, 160, 0)
        ov[:, pl.ds(c * 128, 128)] = block(OFF_V, 160, 0)
        for j in range(8):
            og[:, pl.ds(c * 1024 + j * 128, 128)] = block(OFF_G, 160, j)
            ou[:, pl.ds(c * 1024 + j * 128, 128)] = block(OFF_U, 160, j)
        for j in range(5):
            oo[pl.ds(c * 128, 128), pl.ds(j * 128, 128)] = block(OFF_O, 128, j)
            od[pl.ds(c * 256, 256), pl.ds(j * 128, 128)] = block(OFF_D, 256, j)
    ogain[...] = full[0, pl.ds(OFF_GAIN, 16), :].astype(F32)


def unpack(full):
    def s(*shape):
        return jax.ShapeDtypeStruct(shape, F32)

    return pl.pallas_call(
        unpack_kernel,
        out_shape=(s(160, 1024), s(160, 256), s(160, 256), s(256, 640), s(160, 2048), s(160, 2048), s(512, 640), s(16, 128)),
        in_specs=[VSPEC],
        out_specs=[VSPEC] * 8,
        compiler_params=pltpu.CompilerParams(vmem_limit_bytes=VMEM_LIMIT),
        name="unpack",
    )(full)


def rms(v):
    return lax.rsqrt(jnp.mean(v * v, axis=-1, keepdims=True) + EPS)


def norm_back(v, r, g, u):
    ug = u * g
    return r * ug - v * (r * r * r) * jnp.mean(ug * v, axis=-1, keepdims=True)


def gain_grad(v, r, u):
    return jnp.sum(u * v * r, axis=0, keepdims=True)


def rope(u, cos, sin):
    a, b = u[:, :128], u[:, 128:]
    return jnp.concatenate([a * cos - b * sin, b * cos + a * sin], axis=1)


def rope_back(w, cos, sin):
    a, b = w[:, :128], w[:, 128:]
    return jnp.concatenate([a * cos + b * sin, b * cos - a * sin], axis=1)


def project_kernel(tokens, g_in, w, g_q, g_k, cos, sin, q, k, v, normed_out, raw):
    t = tokens[...].astype(F32)
    normed = (t * rms(t) * g_in[...]).astype(BF)
    normed_out[...] = normed
    weights = w[...].reshape(640, 1536)
    both = dot(normed, weights)
    raw[...] = both[:, :1280]
    for h in range(4):
        u = both[:, h * 256 : h * 256 + 256]
        q[pl.ds(h * 128, 128), :] = (rope(u * rms(u) * g_q[...], cos[...], sin[...]).astype(BF) * 0.0625).astype(BF)
    u = both[:, 1024:1280]
    k[...] = rope(u * rms(u) * g_k[...], cos[...], sin[...]).astype(BF)
    v[...] = both[:, 1280:1536].astype(BF)


def project(tokens, g_in, w, g_q, g_k, cos, sin):
    def s(dtype, *shape):
        return jax.ShapeDtypeStruct(shape, dtype)

    return pl.pallas_call(
        project_kernel,
        out_shape=(s(BF, 512, 256), s(BF, 128, 256), s(BF, 128, 256), s(BF, 128, 640), s(F32, 128, 1280)),
        in_specs=[VSPEC] * 7,
        out_specs=[VSPEC] * 5,
        compiler_params=pltpu.CompilerParams(vmem_limit_bytes=VMEM_LIMIT),
        name="project",
    )(tokens, g_in, w, g_q, g_k, cos, sin)


def causal(x, c_key):
    me = lax.axis_index("ctx")
    start = lax.rem(me, 8) * 128
    row = lax.broadcasted_iota(jnp.int32, (512, 512), 0)
    col = lax.broadcasted_iota(jnp.int32, (512, 512), 1)
    q_pos = start + (row & 127)
    k_pos = (col >> 7) * 256 + c_key * 128 + (col & 127)
    return k_pos <= q_pos


def main_kernel(
    q, k_all, v_all, tokens, cot, w_gu, w_o, w_d, g_post, g_pre, g_fpost,
    layer_out, hidden_grad_out, dq_out, dk, dv, attn_out, projg_out, ffn_out, gug_out, mixed_out, downg_out,
    gg_post, gg_pre, gg_fpost,
    acc, row_sum, gate_s, up_s,
):
    z = lax.div(lax.axis_index("ctx"), 8)
    queries = q[...]
    acc[...] = jnp.zeros_like(acc)
    row_sum[...] = jnp.zeros_like(row_sum)

    def keys_of(c, j):
        return k_all[c, j].reshape(512, 256), v_all[c, j].reshape(512, 256)

    def fwd(c, j, diagonal):
        kt, vt = keys_of(c, j)
        p = jnp.exp(dot_back(queries, kt))
        if diagonal:
            p = jnp.where(causal(None, c), p, 0.0)
        row_sum[...] += jnp.sum(p, axis=1, keepdims=True)
        acc[...] += dot(p.astype(BF), vt)

    def fwd_step(i, _):
        fwd(lax.rem(i, 2), lax.div(i, 2), False)
        return 0

    lax.fori_loop(0, z * 2, fwd_step, 0)
    fwd(0, z, True)
    fwd(1, z, True)
    inv = 1.0 / row_sum[...]
    row_sum[...] = inv
    attended = acc[...] * inv
    acc[...] = attended
    attn = jnp.concatenate([attended[h * 128 : h * 128 + 128] for h in range(4)], axis=1).astype(BF)
    attn_out[...] = attn
    wo = w_o[...].reshape(1024, 640)
    wd = w_d[...].reshape(2048, 640)
    gu = w_gu.reshape(640, 4096)
    proj = dot(attn, wo)
    r_proj = rms(proj)
    hidden = tokens[...].astype(F32) + proj * r_proj * g_post[...]
    r_hidden = rms(hidden)
    ffn = (hidden * r_hidden * g_pre[...]).astype(BF)
    ffn_out[...] = ffn
    for i in range(4):
        cs = pl.ds(i * 512, 512)
        gate = dot(ffn, gu[:, cs])
        up = dot(ffn, gu[:, pl.ds(2048 + i * 512, 512)])
        t = jnp.tanh(C_ROOT * (gate + C_CUBE * gate * gate * gate))
        gelu = 0.5 * gate * (1.0 + t)
        slope = 0.5 * (1.0 + t) + 0.5 * gate * (1.0 - t * t) * (C_ROOT * (1.0 + 3.0 * C_CUBE * gate * gate))
        mixed_out[:, cs] = (gelu * up).astype(BF)
        gate_s[:, cs] = up * slope
        up_s[:, cs] = gelu
    down = dot(mixed_out[...], wd)
    r_down = rms(down)
    layer_out[...] = (hidden + down * r_down * g_fpost[...]).astype(BF)
    out_grad = cot[...].astype(F32)
    down_grad = norm_back(down, r_down, g_fpost[...], out_grad).astype(BF)
    gg_fpost[...] = gain_grad(down, r_down, out_grad)
    downg_out[...] = down_grad
    for i in range(4):
        cs = pl.ds(i * 512, 512)
        mg = dot_back(down_grad, wd[i * 512 : i * 512 + 512])
        gug_out[:, cs] = (mg * gate_s[:, cs]).astype(BF)
        gug_out[:, pl.ds(2048 + i * 512, 512)] = (mg * up_s[:, cs]).astype(BF)
    ffn_grad = dot_back(gug_out[...], gu[...])
    hidden_grad = out_grad + norm_back(hidden, r_hidden, g_pre[...], ffn_grad)
    gg_pre[...] = gain_grad(hidden, r_hidden, ffn_grad)
    hidden_grad_out[...] = hidden_grad
    proj_grad = norm_back(proj, r_proj, g_post[...], hidden_grad).astype(BF)
    gg_post[...] = gain_grad(proj, r_proj, hidden_grad)
    projg_out[...] = proj_grad
    attn_grad = dot_back(proj_grad, wo).astype(BF)
    do = jnp.concatenate([attn_grad[:, h * 256 : h * 256 + 256] for h in range(4)], axis=0)
    delta = jnp.sum(do.astype(F32) * acc[...], axis=1, keepdims=True)
    acc[...] = jnp.zeros_like(acc)

    def bwd(c, j, diagonal):
        kt, vt = keys_of(c, j)
        p = jnp.exp(dot_back(queries, kt)) * row_sum[...]
        if diagonal:
            p = jnp.where(causal(None, c), p, 0.0)
        ds = (p * (dot_back(do, vt) - delta)).astype(BF)
        acc[...] += dot(ds, kt)
        dk[c, j] = tdot(ds, queries).astype(BF).reshape(4, 128, 256)
        dv[c, j] = tdot(p.astype(BF), do).astype(BF).reshape(4, 128, 256)

    def bwd_step(i, _):
        bwd(lax.rem(i, 2), lax.div(i, 2), False)
        return 0

    def zero_step(i, _):
        zero = jnp.zeros((4, 128, 256), BF)
        dk[lax.rem(i, 2), lax.div(i, 2)] = zero
        dv[lax.rem(i, 2), lax.div(i, 2)] = zero
        return 0

    lax.fori_loop(0, z * 2, bwd_step, 0)
    bwd(0, z, True)
    bwd(1, z, True)
    lax.fori_loop(z * 2 + 2, 8, zero_step, 0)
    dq_out[...] = acc[...] * 0.0625


def main_part(q, k_all, v_all, tokens, cot, w_gu, w_o, w_d, g_post, g_pre, g_fpost):
    def s(dtype, *shape):
        return jax.ShapeDtypeStruct(shape, dtype)

    return pl.pallas_call(
        main_kernel,
        out_shape=(
            s(BF, 128, 640), s(F32, 128, 640), s(F32, 512, 256), s(BF, 2, 4, 4, 128, 256), s(BF, 2, 4, 4, 128, 256),
            s(BF, 128, 1024), s(BF, 128, 640), s(BF, 128, 640), s(BF, 128, 4096), s(BF, 128, 2048), s(BF, 128, 640),
            s(F32, 1, 640), s(F32, 1, 640), s(F32, 1, 640),
        ),
        in_specs=[VSPEC] * 11,
        out_specs=[VSPEC] * 14,
        scratch_shapes=[VMEM((512, 256), F32), VMEM((512, 1), F32), VMEM((128, 2048), F32), VMEM((128, 2048), F32)],
        compiler_params=pltpu.CompilerParams(vmem_limit_bytes=VMEM_LIMIT),
        name="main_part",
    )(q, k_all, v_all, tokens, cot, w_gu, w_o, w_d, g_post, g_pre, g_fpost)


def finish_kernel(
    dq, dk, dv, raw, cos, sin, g_q, g_k, w, tokens, g_in, hidden_grad,
    input_grad, qkvg, gg_q, gg_k, gg_in,
):
    total_q = jnp.zeros((1, 256), F32)
    for h in range(4):
        v = raw[:, pl.ds(h * 256, 256)]
        r = rms(v)
        u = rope_back(dq[pl.ds(h * 128, 128), :], cos[...], sin[...])
        total_q += gain_grad(v, r, u)
        qkvg[:, pl.ds(h * 256, 256)] = norm_back(v, r, g_q[...], u).astype(BF)
    gg_q[...] = total_q
    v = raw[:, pl.ds(1024, 256)]
    r = rms(v)
    u = rope_back(dk[...], cos[...], sin[...])
    gg_k[...] = gain_grad(v, r, u)
    qkvg[:, pl.ds(1024, 256)] = norm_back(v, r, g_k[...], u).astype(BF)
    qkvg[:, pl.ds(1280, 256)] = dv[...].astype(BF)
    normed_grad = dot_back(qkvg[...], w[...].reshape(640, 1536))
    t = tokens[...].astype(F32)
    r = rms(t)
    gg_in[...] = gain_grad(t, r, normed_grad)
    input_grad[...] = hidden_grad[...] + norm_back(t, r, g_in[...], normed_grad)


def finish(*args):
    def s(dtype, *shape):
        return jax.ShapeDtypeStruct(shape, dtype)

    return pl.pallas_call(
        finish_kernel,
        out_shape=(s(F32, 128, 640), s(BF, 128, 1536), s(F32, 1, 256), s(F32, 1, 256), s(F32, 1, 640)),
        in_specs=[VSPEC] * 12,
        out_specs=[VSPEC] * 5,
        compiler_params=pltpu.CompilerParams(vmem_limit_bytes=VMEM_LIMIT),
        name="finish",
    )(*args)


GAIN_SIZES = (160, 64, 64, 160, 160, 160)


def local(
    tokens, positions, w_query, w_key, w_value, w_out, w_gate, w_up, w_down,
    gain_in, gain_query, gain_key, gain_attn_post, gain_ffn_pre, gain_ffn_post, cotangent,
):
    gains = jnp.concatenate(
        [gain_in, gain_query, gain_key, gain_attn_post, gain_ffn_pre, gain_ffn_post, jnp.zeros((1280,), BF)]
    ).reshape(16, 128)
    w_qkv, w_gu, w_o, w_d, gain_all = gather_weights(w_query, w_key, w_value, w_out, w_gate, w_up, w_down, gains)
    flat = gain_all.reshape(4, 2048).astype(F32)
    parts, start = [], 0
    for n in GAIN_SIZES:
        parts.append(flat[:, start : start + n].reshape(1, 4 * n))
        start += n
    g_in, g_q, g_k, g_post, g_pre, g_fpost = parts
    exponents = jnp.arange(0, 256, 2, dtype=F32) / 256
    inverse = 1.0 / ROPE_BASE**exponents
    angles = positions.astype(F32)[:, None] * inverse[None, :]
    cos, sin = jnp.cos(angles), jnp.sin(angles)
    q, k, v, normed, raw = project(tokens, g_in, w_qkv, g_q, g_k, cos, sin)
    k_all, v_all = gather_keys(k, v)
    (
        layer_out, hidden_grad, dq, dk, dv, attn, projg, ffn, gug, mixed, downg, gg_post, gg_pre, gg_fpost,
    ) = main_part(q, k_all, v_all, tokens, cotangent, w_gu, w_o, w_d, g_post, g_pre, g_fpost)
    dk_own, dv_own = reduce_key_grads(dk, dv)
    input_grad, qkvg, gg_q, gg_k, gg_in = finish(
        dq, dk_own, dv_own, raw, cos, sin, g_q, g_k, w_qkv, tokens, g_in, hidden_grad
    )
    gain_grads = jnp.concatenate(
        [a.reshape(4, n) for a, n in zip((gg_in, gg_q, gg_k, gg_post, gg_pre, gg_fpost), GAIN_SIZES)]
        + [jnp.zeros((4, 1280), F32)],
        axis=1,
    ).reshape(4, 16, 128)
    full = reduce_weight_grads((normed, qkvg, attn, projg, ffn, gug, mixed, downg), gain_grads)
    oq, ok, ov, oo, og, ou, od, ogain = unpack(full)
    flat = ogain.reshape(2048)
    outs, start = [], 0
    for n in GAIN_SIZES:
        outs.append(flat[start : start + n])
        start += n
    return (layer_out, input_grad, oq, ok, ov, oo, og, ou, od, *outs)


def solution(mesh):
    rows, both, vec = P("fsdp", None), P(("fsdp", "ctx"), None), P("fsdp")
    in_specs = (both, P(("fsdp", "ctx")), *[rows] * 7, *[vec] * 6, both)
    out_specs = (both, both, *[rows] * 7, *[vec] * 6)
    return jax.shard_map(local, mesh=mesh, in_specs=in_specs, out_specs=out_specs, check_vma=False)
```

```python
import functools

import jax
import jax.numpy as jnp
from jax import lax
from jax.experimental import pallas as pl
from jax.experimental.pallas import tpu as pltpu
from jax.sharding import PartitionSpec as P

EPS = 1e-06
ROPE_BASE = 1000000.0
BF = jnp.bfloat16
F32 = jnp.float32
MESH = pl.DeviceIdType.MESH
VMEM = pltpu.VMEM
VSPEC = pl.BlockSpec(memory_space=pltpu.VMEM)
ANYSPEC = pl.BlockSpec(memory_space=pl.ANY)
VMEM_LIMIT = 60 * 1024 * 1024
C_ROOT = 0.7978845608028654
C_CUBE = 0.044715

E_ROWS, M_ROWS, L_ROWS = 4608, 768, 512
OFF_G, OFF_U, OFF_O, OFF_D, E_END = 0, 1280, 2560, 3200, 4480
OFF_Q, M_END = 0, 640
OFF_K, OFF_V, OFF_GAIN, L_END = 0, 160, 320, 336
EA_PARTS = ((0, 2560, "yzx"),)
EB_PARTS = ((2560, 1024, "xzy"), (3584, 1024, "zxy"))
M_PARTS = ((0, 256, "yzx"), (256, 256, "xzy"), (512, 256, "zxy"))
L_PARTS = ((0, 256, "yzx"), (256, 256, "xyz"))
GAIN_SIZES = (160, 64, 64, 160, 160, 160)
STEPS = (2, 1, -1)


class Net:
    def __init__(self, send_sem, recv_sem):
        me = lax.axis_index("ctx")
        self.y = lax.axis_index("fsdp")
        self.c = lax.rem(me, 2)
        self.x = lax.rem(lax.div(me, 2), 4)
        self.z = lax.div(me, 8)
        self.send_sem, self.recv_sem = send_sem, recv_sem
        self.used = 0
        self.sent = []

    def pos(self, axis):
        return {"x": self.x, "y": self.y, "z": self.z}[axis]

    def at(self, axis, step):
        return lax.rem(self.pos(axis) + (step + 4), 4)

    def dev(self, axis, step):
        x, y, z, c = self.x, self.y, self.z, self.c
        if axis == "x":
            x = self.at("x", step)
        elif axis == "y":
            y = self.at("y", step)
        elif axis == "z":
            z = self.at("z", step)
        else:
            c = 1 - c
        return {"fsdp": y, "ctx": z * 8 + x * 2 + c}

    def copy(self, src, dst, axis, step=1):
        k = self.used
        self.used += 1
        cp = pltpu.make_async_remote_copy(
            src_ref=src,
            dst_ref=dst,
            send_sem=self.send_sem.at[k],
            recv_sem=self.recv_sem.at[k],
            device_id=self.dev(axis, step),
            device_id_type=MESH,
        )
        cp.start()
        self.sent.append(cp)
        return cp

    def barrier(self):
        sem = pltpu.get_barrier_semaphore()
        peers = [("c", 1), *[(a, s) for a in "xyz" for s in STEPS]]
        for axis, step in peers:
            pl.semaphore_signal(sem, inc=1, device_id=self.dev(axis, step), device_id_type=MESH)
        pl.semaphore_wait(sem, len(peers))

    def drain(self):
        for cp in self.sent:
            cp.wait_send()


class Relay:
    def __init__(self, net, axis, piece, own):
        self.net, self.axis, self.piece, self.own = net, axis, piece, own

    def start(self):
        self.up = [self.net.copy(a, b, self.axis, 1) for a, b in self.own]
        self.down = [self.net.copy(a, b, self.axis, -1) for a, b in self.own]

    def mid(self):
        for cp in self.up:
            cp.wait_recv()
        low = self.piece(self.net.at(self.axis, -1), 0)
        self.up2 = self.net.copy(low, low, self.axis, 1)
        for cp in self.down:
            cp.wait_recv()
        high = self.piece(self.net.at(self.axis, 1), 1)
        self.down2 = self.net.copy(high, high, self.axis, -1)

    def end(self):
        self.up2.wait_recv()
        self.down2.wait_recv()


class Gather:
    def __init__(self, net, axis, piece):
        self.net, self.axis, self.piece = net, axis, piece

    def start(self):
        own = self.piece(self.net.pos(self.axis))
        self.copies = [(s, self.net.copy(own, own, self.axis, s)) for s in (1, -1, 2)]

    def end(self, then=None):
        for s, cp in self.copies:
            cp.wait_recv()
            if then is not None:
                then(self.net.at(self.axis, -s))


class Scatter:
    def __init__(self, net, axis, q, bufs):
        self.net, self.axis, self.q, self.bufs = net, axis, q, bufs
        self.copies = []

    def send(self, s):
        buf = self.bufs[STEPS.index(s)]
        self.copies.append(self.net.copy(self.q(self.net.at(self.axis, s)), buf, self.axis, s))

    def start(self):
        for s in STEPS:
            self.send(s)

    def end(self, out=None):
        for cp in self.copies:
            cp.wait_recv()
        add_rows(self.q(self.net.pos(self.axis)), self.bufs, out)


def add_rows(dst, srcs, out=None):
    target = dst if out is None else out
    lead, rows = dst.shape[:-2], dst.shape[-2]
    step = next(n for n in (256, 192, 128, 96, 64, 48, 32, 16) if rows % n == 0)
    per = rows // step
    count = per
    for n in lead:
        count *= n

    def body(i, _):
        idx = []
        k = lax.div(i, per)
        for n in reversed(lead):
            idx.insert(0, lax.rem(k, n))
            k = lax.div(k, n)
        idx = (*idx, pl.ds(pl.multiple_of(lax.rem(i, per) * step, 16), step), slice(None))
        total = dst[idx].astype(F32)
        for s in srcs:
            total += s[idx].astype(F32)
        target[idx] = total.astype(target.dtype)
        return 0

    lax.fori_loop(0, count, body, 0)


def tdot(a, b):
    return lax.dot_general(a, b, (((0,), (0,)), ((), ())), preferred_element_type=F32)


def dot(a, b):
    return jnp.dot(a, b, preferred_element_type=F32)


def dot_back(a, b):
    return lax.dot_general(a, b, (((1,), (1,)), ((), ())), preferred_element_type=F32)


def rms(v):
    return lax.rsqrt(jnp.mean(v * v, axis=-1, keepdims=True) + EPS)


def norm_back(v, r, g, u):
    ug = u * g
    return r * ug - v * (r * r * r) * jnp.mean(ug * v, axis=-1, keepdims=True)


def gain_grad(v, r, u):
    return jnp.sum(u * v * r, axis=0, keepdims=True)


def rope(u, cos, sin):
    a, b = u[:, :128], u[:, 128:]
    return jnp.concatenate([a * cos - b * sin, b * cos + a * sin], axis=1)


def rope_back(w, cos, sin):
    a, b = w[:, :128], w[:, 128:]
    return jnp.concatenate([a * cos + b * sin, b * cos - a * sin], axis=1)


def causal(net, c_key):
    row = lax.broadcasted_iota(jnp.int32, (512, 512), 0)
    col = lax.broadcasted_iota(jnp.int32, (512, 512), 1)
    q_pos = (net.x * 2 + net.c) * 128 + (row & 127)
    k_pos = (col >> 7) * 256 + c_key * 128 + (col & 127)
    return k_pos <= q_pos


class Group:
    def __init__(self, net, g, full, parts, bufs):
        self.net, self.g, self.full, self.parts, self.bufs = net, g, full, parts, bufs
        self.place = [[0, 4, off, rows] for off, rows, _ in parts]
        self.phase = -1

    def q(self, p, axis):
        y0, yn, r0, rn = self.place[p]

        def share(j):
            if axis == "y":
                return self.g.at[pl.ds(j, 1), pl.ds(pl.multiple_of(r0, 16), rn)]
            return self.g.at[pl.ds(y0, yn), pl.ds(pl.multiple_of(r0 + j * (rn // 4), 16), rn // 4)]

        return share

    def scatter_start(self, phase):
        self.runs = []
        for p, (_, _, order) in enumerate(self.parts):
            k = (p * 3 + phase) * 3
            self.runs.append(Scatter(self.net, order[phase], self.q(p, order[phase]), self.bufs[k : k + 3]))
            self.runs[-1].start()

    def scatter_end(self, phase):
        for p, r in enumerate(self.runs):
            y0, yn, r0, rn = self.place[p]
            axis = self.parts[p][2][phase]
            if axis == "y":
                self.place[p] = [self.net.y, 1, r0, rn]
            else:
                self.place[p] = [y0, yn, r0 + self.net.pos(axis) * (rn // 4), rn // 4]
            _, _, r0, rn = self.place[p]
            r.end(self.full.at[pl.ds(self.net.c, 1), pl.ds(pl.multiple_of(r0, 16), rn)] if phase == 2 else None)

    def gather_start(self, stage):
        self.runs = []
        for off, rows, order in self.parts:
            u = rows // 16
            major, minor = order.replace("y", "")

            def piece(j, u=u, off=off, major=major):
                if stage == 0:
                    return self.full.at[self.net.c, pl.ds(pl.multiple_of(off + self.net.pos(major) * 4 * u + j * u, 16), u)]
                return self.full.at[self.net.c, pl.ds(pl.multiple_of(off + j * 4 * u, 16), 4 * u)]

            self.runs.append(Gather(self.net, minor if stage == 0 else major, piece))
            self.runs[-1].start()

    def step(self):
        done, self.phase = self.phase, self.phase + 1
        if 0 <= done < 3:
            self.scatter_end(done)
        elif 3 <= done < 5:
            for r in self.runs:
                r.end()
        elif done == 5:
            self.swap.wait_recv()
        if done < 2:
            self.scatter_start(done + 1)
        elif done < 4:
            self.gather_start(done - 2)
        elif done == 4:
            ref = self.full.at[self.net.c, pl.ds(self.parts[0][0], sum(rows for _, rows, _ in self.parts))]
            self.swap = self.net.copy(ref, ref, "c")


def group_bufs(parts):
    bufs = []
    for _, rows, order in parts:
        lead = 4
        for axis in order:
            if axis == "y":
                lead = 1
            else:
                rows //= 4
            bufs += [VMEM((lead, rows, 128), BF)] * 3
    return bufs


ALL_PARTS = (EA_PARTS, EB_PARTS, M_PARTS, L_PARTS)


def layer_kernel(*refs):
    refs = list(refs)

    def take_refs(n):
        out = refs[:n]
        del refs[:n]
        return out

    wq, wk, wv, wo, wg, wu, wd = take_refs(7)
    gain_ins = take_refs(6)
    tokens, cot, cos, sin = take_refs(4)
    layer_out, input_grad, e_full, m_full, l_full = take_refs(5)
    qkv_all, gu, wo_all, wd_all, k_all, v_all = take_refs(6)
    normed, qkvg, attn, projg, ffn, gug, mixed, downg = take_refs(8)
    gain_all, gains, gain_s, gain_other, ge, gm, gl = take_refs(7)
    dk, dv, kin, vin, acc, inv_s, delta_s, do_s, q_s, raw, f_s, g_s, hidden_grad_s = take_refs(13)
    kbufs, vbufs, k2bufs, v2bufs = take_refs(3), take_refs(3), take_refs(3), take_refs(3)
    group_b = [take_refs(9 * len(parts)) for parts in ALL_PARTS]
    send_sem, recv_sem, own_sem = take_refs(3)
    net = Net(send_sem, recv_sem)
    y, c, x, z = net.y, net.c, net.x, net.z
    other = 1 - c
    own_rows, other_rows = pl.ds(0, 128), pl.ds(128, 128)
    own = []
    for k, (src, dst) in enumerate(
        [
            (wg, gu.at[y, :, pl.ds(0, 2048)]), (wu, gu.at[y, :, pl.ds(2048, 2048)]),
            (wq, qkv_all.at[y, :, pl.ds(0, 1024)]), (wk, qkv_all.at[y, :, pl.ds(1024, 256)]),
            (wv, qkv_all.at[y, :, pl.ds(1280, 256)]), (wo, wo_all.at[y]), (wd, wd_all.at[y]),
        ]
    ):
        own.append(pltpu.make_async_copy(src, dst, own_sem.at[k]))
        own[-1].start()
    gain_all[y] = jnp.zeros((8, 256), F32)
    for i, n in enumerate(GAIN_SIZES):
        gain_all[y, pl.ds(i, 1), pl.ds(0, n)] = gain_ins[i][...].astype(F32)
    net.barrier()
    for cp in own:
        cp.wait()

    rows = pl.ds(pl.multiple_of(c * 80, 16), 80)

    def block(yq, start, n):
        return gu.at[yq, rows, pl.ds(pl.multiple_of(start, 128), n)]

    def gate_one(yq, xj, zj):
        return block(yq, (zj * 4 + xj) * 128, 128)

    def up_one(yq, xj, zj):
        return block(yq, 2048 + (xj * 4 + zj) * 128, 128)

    def qkv_piece(yq, half=None):
        off, n = {None: (0, 1536), 0: (0, 768), 1: (768, 768)}[half]
        return qkv_all.at[yq, rows, pl.ds(off, n)]

    def gu_piece(yq):
        return gu.at[yq, rows]

    def row_piece(ref, size):
        def piece(yq, half=None):
            off, n = {None: (0, size), 0: (0, size // 2), 1: (size // 2, size // 2)}[half]
            return ref.at[yq, pl.ds(pl.multiple_of(c * size + off, 16), n)]

        return piece

    wo_piece, wd_piece = row_piece(wo_all, 128), row_piece(wd_all, 256)
    gu_y = [Gather(net, "y", lambda j: gate_one(j, x, z)), Gather(net, "y", lambda j: up_one(j, x, z))]
    for g in gu_y:
        g.start()
    qkv = Relay(net, "y", qkv_piece, [(qkv_piece(y), qkv_piece(y))])
    w_o = Relay(net, "y", wo_piece, [(wo_piece(y), wo_piece(y))])
    w_d = Relay(net, "y", wd_piece, [(wd_piece(y), wd_piece(y))])
    qkv.start()
    gain_own = gain_all.at[y]
    gain_copies = [net.copy(gain_own, gain_own, "y", s) for s in STEPS]
    for g in gu_y:
        g.end()
    gu_1, gu_2 = [], []
    for s in (1, -1, 2):
        yq = net.at("y", s)
        gu_1.append(Gather(net, "x", lambda j, yq=yq: gate_one(yq, j, z)))
        gu_1.append(Gather(net, "z", lambda j, yq=yq: up_one(yq, x, j)))
        gu_2.append(Gather(net, "z", lambda j, yq=yq: block(yq, j * 512, 512)))
        gu_2.append(Gather(net, "x", lambda j, yq=yq: block(yq, 2048 + j * 512, 512)))
    for g in gu_1:
        g.start()
    for cp in gain_copies:
        cp.wait_recv()
    all_gains = gain_all[...]

    def gain(i, n):
        return jnp.concatenate([all_gains[yq, i : i + 1, :n] for yq in range(4)], axis=1)

    gains[0:1, :] = gain(0, 160)
    for i in range(3, 6):
        gains[i : i + 1, :] = gain(i, 160)
    gains[1:2, 0:256] = gain(1, 64)
    gains[2:3, 0:256] = gain(2, 64)
    g_in, g_q, g_k = gains[0:1, :], gains[1:2, 0:256], gains[2:3, 0:256]
    g_post, g_pre, g_fpost = gains[3:4, :], gains[4:5, :], gains[5:6, :]
    t = tokens[...].astype(F32)
    normed_low = (t * rms(t) * g_in).astype(BF)
    normed[own_rows, :] = normed_low

    def share(ref):
        return net.copy(ref.at[own_rows], ref.at[other_rows], "c")

    swaps = {}

    def swap(name, piece, j):
        swaps.setdefault(name, []).append(net.copy(piece(j), piece(j), "c"))

    def swapped(name):
        for cp in swaps[name]:
            cp.wait_recv()

    qkv.mid()
    w_o.start()
    w_d.start()
    swap("qkv", qkv_piece, net.at("y", 1))
    swap("qkv", qkv_piece, net.at("y", -1))
    for a, b in zip(gu_1, gu_2):
        a.end()
    for b in gu_2:
        b.start()
    qkv.end()
    swap("qkv", qkv_piece, net.at("y", 2))
    swapped("qkv")
    both = dot(normed_low, qkv_all[:, :, pl.ds(1024, 512)].reshape(640, 512))
    u = both[:, 0:256]
    raw[:, pl.ds(1024, 256)] = u
    k_all[c, z, x] = rope(u * rms(u) * g_k, cos[...], sin[...]).astype(BF)
    v_all[c, z, x] = both[:, 256:512].astype(BF)
    kx = Gather(net, "x", lambda j: k_all.at[c, z, j])
    vz = Gather(net, "z", lambda j: v_all.at[c, j, x])
    kz = Gather(net, "z", lambda j: k_all.at[c, j])
    vx = Gather(net, "x", lambda j: v_all.at[c, :, j])
    kx.start()
    vz.start()
    both = dot(normed_low, qkv_all[:, :, pl.ds(0, 1024)].reshape(640, 1024))
    raw[:, pl.ds(0, 1024)] = both
    for h in range(4):
        u = both[:, h * 256 : h * 256 + 256]
        q_s[pl.ds(h * 128, 128), :] = (rope(u * rms(u) * g_q, cos[...], sin[...]).astype(BF) * 0.0625).astype(BF)

    def swap_k(j):
        swap("kv", lambda j: k_all.at[c, j], j)

    def swap_v(j):
        swap("kv", lambda j: v_all.at[c, :, j], j)

    kx.end()
    kz.start()
    vz.end()
    vx.start()
    swap_k(z)
    swap_v(x)
    acc[...] = jnp.zeros_like(acc)
    inv_s[...] = jnp.zeros_like(inv_s)
    gain_s[...] = jnp.zeros_like(gain_s)
    ge[:, pl.ds(E_END, E_ROWS - E_END), :] = jnp.zeros((4, E_ROWS - E_END, 128), BF)
    gm[:, pl.ds(M_END, M_ROWS - M_END), :] = jnp.zeros((4, M_ROWS - M_END, 128), BF)
    gl[:, pl.ds(L_END, L_ROWS - L_END), :] = jnp.zeros((4, L_ROWS - L_END, 128), BF)
    shared = {"normed": share(normed)}
    w_o.mid()
    w_d.mid()
    for name, piece in (("wo", wo_piece), ("wd", wd_piece)):
        swap(name, piece, net.at("y", 1))
        swap(name, piece, net.at("y", -1))
    for g in gu_2:
        g.end()
    for s in (1, -1, 2):
        swap("gu", gu_piece, net.at("y", s))
    kz.end(swap_k)
    vx.end(swap_v)
    for r, name, piece in ((w_o, "wo", wo_piece), (w_d, "wd", wd_piece)):
        r.end()
        swap(name, piece, net.at("y", 2))
    swapped("kv")

    def fwd_tile(cc, j, diagonal):
        p = jnp.exp(dot_back(q_s[...], k_all[cc, j].reshape(512, 256)))
        if diagonal:
            p = jnp.where(causal(net, cc), p, 0.0)
        inv_s[...] += jnp.sum(p, axis=1, keepdims=True)
        acc[...] += dot(p.astype(BF), v_all[cc, j].reshape(512, 256))

    def fwd_step(i, _):
        fwd_tile(lax.rem(i, 2), lax.div(i, 2), False)
        return 0

    def fwd_last(i, _):
        fwd_tile(i, z, True)
        return 0

    lax.fori_loop(0, z * 2, fwd_step, 0)
    lax.fori_loop(0, 2, fwd_last, 0)
    inv = 1.0 / inv_s[...]
    inv_s[...] = inv
    acc[...] = acc[...] * inv
    for h in range(4):
        attn[own_rows, pl.ds(h * 256, 256)] = acc[pl.ds(h * 128, 128), :].astype(BF)
    shared["attn"] = share(attn)

    def put_gain(i, value):
        n = value.shape[1] // 4
        for yq in range(4):
            v = value[:, yq * n : yq * n + n]
            gain_s[yq, pl.ds(2 * i, 1), pl.ds(0, min(n, 128))] = v[:, :128]
            if n > 128:
                gain_s[yq, pl.ds(2 * i + 1, 1), pl.ds(0, n - 128)] = v[:, 128:]

    swapped("wo")
    w_out = wo_all[...].reshape(1024, 640)
    proj = dot(attn[own_rows, :], w_out)
    r_proj = rms(proj)
    hidden = tokens[...].astype(F32) + proj * r_proj * g_post
    r_hidden = rms(hidden)
    ffn_low = (hidden * r_hidden * g_pre).astype(BF)
    ffn[own_rows, :] = ffn_low
    shared["ffn"] = share(ffn)
    swapped("gu")
    for i in range(4):
        cs, cs2 = pl.ds(i * 512, 512), pl.ds(2048 + i * 512, 512)
        gate = dot(ffn_low, gu[:, :, cs].reshape(640, 512))
        up = dot(ffn_low, gu[:, :, cs2].reshape(640, 512))
        t = jnp.tanh(C_ROOT * (gate + C_CUBE * gate * gate * gate))
        gelu = 0.5 * gate * (1.0 + t)
        slope = 0.5 * (1.0 + t) + 0.5 * gate * (1.0 - t * t) * (C_ROOT * (1.0 + 3.0 * C_CUBE * gate * gate))
        mixed[own_rows, cs] = (gelu * up).astype(BF)
        f_s[:, cs] = up * slope
        g_s[:, cs] = gelu
    shared["mixed"] = share(mixed)
    swapped("wd")
    down = dot(mixed[own_rows, :], wd_all[...].reshape(2048, 640))
    r_down = rms(down)
    layer_out[...] = (hidden + down * r_down * g_fpost).astype(BF)
    out_grad = cot[...].astype(F32)
    down_grad = norm_back(down, r_down, g_fpost, out_grad).astype(BF)
    put_gain(5, gain_grad(down, r_down, out_grad))
    downg[own_rows, :] = down_grad
    shared["downg"] = share(downg)
    for i in range(4):
        cs, cs2 = pl.ds(i * 512, 512), pl.ds(2048 + i * 512, 512)
        mg = dot_back(down_grad, wd_all[i])
        gug[own_rows, cs] = (mg * f_s[:, cs]).astype(BF)
        gug[own_rows, cs2] = (mg * g_s[:, cs]).astype(BF)
    shared["gug"] = share(gug)
    ffn_grad = dot_back(gug[own_rows, :], gu[...].reshape(640, 4096))
    hidden_grad = out_grad + norm_back(hidden, r_hidden, g_pre, ffn_grad)
    put_gain(4, gain_grad(hidden, r_hidden, ffn_grad))
    hidden_grad_s[...] = hidden_grad
    proj_grad = norm_back(proj, r_proj, g_post, hidden_grad).astype(BF)
    put_gain(3, gain_grad(proj, r_proj, hidden_grad))
    projg[own_rows, :] = proj_grad
    shared["projg"] = share(projg)
    attn_grad = dot_back(proj_grad, w_out).astype(BF)
    for h in range(4):
        do_s[pl.ds(h * 128, 128), :] = attn_grad[:, h * 256 : h * 256 + 256]
    delta_s[...] = jnp.sum(do_s[...].astype(F32) * acc[...], axis=1, keepdims=True)

    def cols(start, width):
        return pl.ds(pl.multiple_of(start, 128), width)

    def put(g, off, n, value, col_blocks):
        value = value.astype(BF)
        for yq in range(4):
            for j in range(col_blocks):
                g[yq, pl.ds(off + j * n, n), :] = value[yq * n : yq * n + n, j * 128 : j * 128 + 128]

    for name in ("attn", "ffn", "mixed", "downg", "gug", "projg"):
        shared[name].wait_recv()
    for part in range(2):
        put(ge, OFF_G + part * 640, 160, tdot(ffn[...], gug[:, cols(c * 1024 + part * 512, 512)]), 4)
        put(ge, OFF_U + part * 640, 160, tdot(ffn[...], gug[:, cols(2048 + c * 1024 + part * 512, 512)]), 4)
    early_a = Group(net, ge, e_full, EA_PARTS, group_b[0])
    early_a.step()
    for yq in range(4):
        value = tdot(attn[:, cols(yq * 256 + c * 128, 128)], projg[...]).astype(BF)
        for j in range(5):
            ge[yq, pl.ds(OFF_O + j * 128, 128), :] = value[:, j * 128 : j * 128 + 128]
        value = tdot(mixed[:, cols(yq * 512 + c * 256, 256)], downg[...]).astype(BF)
        for j in range(5):
            ge[yq, pl.ds(OFF_D + j * 256, 256), :] = value[:, j * 128 : j * 128 + 128]
    early_b = Group(net, ge, e_full, EB_PARTS, group_b[1])
    early_b.step()

    acc[...] = jnp.zeros_like(acc)

    def tile(cc, j, diagonal):
        kt, vt = k_all[cc, j].reshape(512, 256), v_all[cc, j].reshape(512, 256)
        p = jnp.exp(dot_back(q_s[...], kt)) * inv_s[...]
        if diagonal:
            p = jnp.where(causal(net, cc), p, 0.0)
        ds = (p * (dot_back(do_s[...], vt) - delta_s[...])).astype(BF)
        acc[...] += dot(ds, kt)
        dk[cc, j] = tdot(ds, q_s[...]).astype(BF).reshape(4, 128, 256)
        dv[cc, j] = tdot(p.astype(BF), do_s[...]).astype(BF).reshape(4, 128, 256)

    kc, vc = {}, {}

    def tiles(s):
        j = net.at("z", s)

        def step(i, _):
            cc = lax.rem(other + i, 2)
            if s == 0:
                tile(cc, j, True)
            else:

                @pl.when(j < z)
                def _():
                    tile(cc, j, False)

                @pl.when(j > z)
                def _():
                    dk[cc, j] = jnp.zeros((4, 128, 256), BF)
                    dv[cc, j] = jnp.zeros((4, 128, 256), BF)

            return 0

        lax.fori_loop(0, 2, step, 0)
        kc[s] = net.copy(dk.at[other, j], kin.at[j], "c")
        vc[s] = net.copy(dv.at[other, j], vin.at[j], "c")

    k1 = Scatter(net, "z", lambda j: kin.at[j], kbufs)
    v1 = Scatter(net, "x", lambda j: vin.at[:, j], vbufs)
    k2 = Scatter(net, "x", lambda j: kin.at[z, j], k2bufs)
    v2 = Scatter(net, "z", lambda j: vin.at[j, x], v2bufs)

    def take(s):
        j = net.at("z", s)
        kc[s].wait_recv()
        add_rows(kin.at[j], (dk.at[c, j],))
        if s != 0:
            k1.send(s)
        vc[s].wait_recv()
        add_rows(vin.at[j], (dv.at[c, j],))

    tiles(2)
    tiles(1)
    take(2)
    tiles(-1)
    take(1)
    tiles(0)
    take(-1)
    take(0)
    v1.start()

    total_q = jnp.zeros((1, 256), F32)
    for h in range(4):
        v = raw[:, pl.ds(h * 256, 256)]
        r = rms(v)
        u = rope_back(acc[pl.ds(h * 128, 128), :] * 0.0625, cos[...], sin[...])
        total_q += gain_grad(v, r, u)
        qkvg[own_rows, pl.ds(h * 256, 256)] = norm_back(v, r, g_q, u).astype(BF)
    put_gain(1, total_q)
    q_cols, kv_cols = pl.ds(0, 1024), pl.ds(1024, 512)
    share_q = net.copy(qkvg.at[own_rows, q_cols], qkvg.at[other_rows, q_cols], "c")
    normed_grad = dot_back(qkvg[own_rows, q_cols], qkv_all[:, :, q_cols].reshape(640, 1024))
    early_b.step()
    shared["normed"].wait_recv()
    share_q.wait_recv()
    put(gm, OFF_Q, 160, tdot(normed[...], qkvg[:, cols(c * 512, 512)]), 4)
    middle = Group(net, gm, m_full, M_PARTS, group_b[2])
    k1.end()
    k2.start()
    v1.end()
    v2.start()
    middle.step()
    early_b.step()
    k2.end()
    v2.end()

    v = raw[:, pl.ds(1024, 256)]
    r = rms(v)
    u = rope_back(kin[z, x].astype(F32), cos[...], sin[...])
    put_gain(2, gain_grad(v, r, u))
    qkvg[own_rows, pl.ds(1024, 256)] = norm_back(v, r, g_k, u).astype(BF)
    qkvg[own_rows, pl.ds(1280, 256)] = vin[z, x]
    share_kv = net.copy(qkvg.at[own_rows, kv_cols], qkvg.at[other_rows, kv_cols], "c")
    normed_grad = normed_grad + dot_back(qkvg[own_rows, kv_cols], qkv_all[:, :, kv_cols].reshape(640, 512))
    t = tokens[...].astype(F32)
    r = rms(t)
    put_gain(0, gain_grad(t, r, normed_grad))
    gain_copy = net.copy(gain_s, gain_other, "c")
    input_grad[...] = hidden_grad_s[...] + norm_back(t, r, g_in, normed_grad)
    middle.step()
    share_kv.wait_recv()
    put(gl, OFF_K, 160, tdot(normed[...], qkvg[:, cols(1024 + c * 128, 128)]), 1)
    put(gl, OFF_V, 160, tdot(normed[...], qkvg[:, cols(1280 + c * 128, 128)]), 1)
    gain_copy.wait_recv()
    gl[:, pl.ds(OFF_GAIN, 16), :] = (gain_s[...] + gain_other[...]).astype(BF)
    late = Group(net, gl, l_full, L_PARTS, group_b[3])
    late.step()
    early_a.step()
    early_b.step()
    middle.step()
    late.step()
    early_a.step()
    early_b.step()
    middle.step()
    late.step()
    early_a.step()
    early_b.step()
    middle.step()
    late.step()
    early_a.step()
    middle.step()
    late.step()
    early_a.step()
    late.step()
    early_b.step()
    middle.step()
    early_a.step()
    late.step()
    net.drain()


def layer(*args):
    def s(dtype, *shape):
        return jax.ShapeDtypeStruct(shape, dtype)

    n = 6 + 4 + 3 + 18 + 18 + 3 + 4 + 4 + 3 + 3 + 3 + 12 + 8 + 8 + 2 + 8 + 12 + sum(16 * len(p) + 1 for p in ALL_PARTS)
    big, small = VMEM((4, 128, 256), BF), VMEM((128, 256), BF)
    whole = VMEM((2, 4, 4, 128, 256), BF)
    column = VMEM((512, 1), F32)
    return pl.pallas_call(
        layer_kernel,
        out_shape=(
            s(BF, 128, 640), s(F32, 128, 640), s(BF, 2, E_ROWS, 128), s(BF, 2, M_ROWS, 128), s(BF, 2, L_ROWS, 128)
        ),
        in_specs=[ANYSPEC] * 7 + [VSPEC] * 10,
        out_specs=[VSPEC] * 5,
        scratch_shapes=[
            VMEM((4, 160, 1536), BF), VMEM((4, 160, 4096), BF), VMEM((4, 256, 640), BF), VMEM((4, 512, 640), BF),
            whole, whole,
            *[VMEM((256, n), BF) for n in (640, 1536, 1024, 640, 640, 4096, 2048, 640)],
            VMEM((4, 8, 256), F32), VMEM((8, 640), F32), VMEM((4, 16, 128), F32), VMEM((4, 16, 128), F32),
            VMEM((4, E_ROWS, 128), BF), VMEM((4, M_ROWS, 128), BF), VMEM((4, L_ROWS, 128), BF),
            whole, whole, VMEM((4, 4, 128, 256), BF), VMEM((4, 4, 128, 256), BF),
            VMEM((512, 256), F32), column, column, VMEM((512, 256), BF), VMEM((512, 256), BF), VMEM((128, 1280), F32),
            VMEM((128, 2048), F32), VMEM((128, 2048), F32), VMEM((128, 640), F32),
            *[big] * 6, *[small] * 6,
            *[b for parts in ALL_PARTS for b in group_bufs(parts)],
            pltpu.SemaphoreType.DMA((n,)),
            pltpu.SemaphoreType.DMA((n,)),
            pltpu.SemaphoreType.DMA((7,)),
        ],
        compiler_params=pltpu.CompilerParams(collective_id=0, has_side_effects=True, vmem_limit_bytes=VMEM_LIMIT),
        name="layer",
    )(*args)


def unpack_kernel(e, m, l, oq, ok, ov, oo, og, ou, od, *gain_outs):
    for c in range(2):

        def block(full, off, n, j):
            return full[c, pl.ds(off + j * n, n), :].astype(F32)

        for j in range(4):
            oq[:, pl.ds(c * 512 + j * 128, 128)] = block(m, OFF_Q, 160, j)
        ok[:, pl.ds(c * 128, 128)] = block(l, OFF_K, 160, 0)
        ov[:, pl.ds(c * 128, 128)] = block(l, OFF_V, 160, 0)
        for j in range(8):
            og[:, pl.ds(c * 1024 + j * 128, 128)] = block(e, OFF_G, 160, j)
            ou[:, pl.ds(c * 1024 + j * 128, 128)] = block(e, OFF_U, 160, j)
        for j in range(5):
            oo[pl.ds(c * 128, 128), pl.ds(j * 128, 128)] = block(e, OFF_O, 128, j)
            od[pl.ds(c * 256, 256), pl.ds(j * 128, 128)] = block(e, OFF_D, 256, j)
    rows = l[0, pl.ds(OFF_GAIN, 16), :].astype(F32)
    for i, n in enumerate(GAIN_SIZES):
        gain_outs[i][:, pl.ds(0, min(n, 128))] = rows[2 * i : 2 * i + 1, : min(n, 128)]
        if n > 128:
            gain_outs[i][:, pl.ds(128, n - 128)] = rows[2 * i + 1 : 2 * i + 2, : n - 128]


def unpack(e, m, l):
    def s(*shape):
        return jax.ShapeDtypeStruct(shape, F32)

    return pl.pallas_call(
        unpack_kernel,
        out_shape=(
            s(160, 1024), s(160, 256), s(160, 256), s(256, 640), s(160, 2048), s(160, 2048), s(512, 640),
            *[s(1, n) for n in GAIN_SIZES],
        ),
        in_specs=[VSPEC] * 3,
        out_specs=[VSPEC] * 13,
        compiler_params=pltpu.CompilerParams(vmem_limit_bytes=VMEM_LIMIT),
        name="unpack",
    )(e, m, l)


def local(
    tokens, positions, w_query, w_key, w_value, w_out, w_gate, w_up, w_down,
    gain_in, gain_query, gain_key, gain_attn_post, gain_ffn_pre, gain_ffn_post, cotangent,
):
    gains = [
        g.reshape(1, g.shape[0]) for g in (gain_in, gain_query, gain_key, gain_attn_post, gain_ffn_pre, gain_ffn_post)
    ]
    exponents = jnp.arange(0, 256, 2, dtype=F32) / 256
    inverse = 1.0 / ROPE_BASE**exponents
    angles = positions.astype(F32)[:, None] * inverse[None, :]
    cos, sin = jnp.cos(angles), jnp.sin(angles)
    layer_out, input_grad, e_full, m_full, l_full = layer(
        w_query, w_key, w_value, w_out, w_gate, w_up, w_down, *gains, tokens, cotangent, cos, sin
    )
    oq, ok, ov, oo, og, ou, od, *gain_grads = unpack(e_full, m_full, l_full)
    return (layer_out, input_grad, oq, ok, ov, oo, og, ou, od, *[g.reshape(g.shape[1]) for g in gain_grads])


def solution(mesh):
    rows, both, vec = P("fsdp", None), P(("fsdp", "ctx"), None), P("fsdp")
    in_specs = (both, P(("fsdp", "ctx")), *[rows] * 7, *[vec] * 6, both)
    out_specs = (both, both, *[rows] * 7, *[vec] * 6)
    return jax.shard_map(local, mesh=mesh, in_specs=in_specs, out_specs=out_specs, check_vma=False)
```

```python
import functools

import jax
import jax.numpy as jnp
from jax import lax
from jax.experimental import pallas as pl
from jax.experimental.pallas import tpu as pltpu
from jax.sharding import PartitionSpec as P

EPS = 1e-06
ROPE_BASE = 1000000.0
BF = jnp.bfloat16
F32 = jnp.float32
MESH = pl.DeviceIdType.MESH
VMEM = pltpu.VMEM
VSPEC = pl.BlockSpec(memory_space=pltpu.VMEM)
ANYSPEC = pl.BlockSpec(memory_space=pl.ANY)
VMEM_LIMIT = 60 * 1024 * 1024
C_ROOT = 0.7978845608028654
C_CUBE = 0.044715

E_ROWS, M_ROWS, L_ROWS = 4608, 768, 512
OFF_G, OFF_U, OFF_O, OFF_D, E_END = 0, 1280, 2560, 3200, 4480
OFF_Q, M_END = 0, 640
OFF_K, OFF_V, OFF_GAIN, L_END = 0, 160, 320, 336
EA_PARTS = ((0, 1280, "yzx"), (1280, 1280, "yxz"))
EB_PARTS = ((2560, 1024, "xzy"), (3584, 1024, "zxy"))
M_PARTS = ((0, 256, "yzx"), (256, 256, "xzy"), (512, 256, "zxy"))
L_PARTS = ((0, 256, "yzx"), (256, 256, "xyz"))
GAIN_SIZES = (160, 64, 64, 160, 160, 160)
STEPS = (2, 1, -1)


class Net:
    def __init__(self, send_sem, recv_sem):
        me = lax.axis_index("ctx")
        self.y = lax.axis_index("fsdp")
        self.c = lax.rem(me, 2)
        self.x = lax.rem(lax.div(me, 2), 4)
        self.z = lax.div(me, 8)
        self.send_sem, self.recv_sem = send_sem, recv_sem
        self.used = 0
        self.sent = []

    def pos(self, axis):
        return {"x": self.x, "y": self.y, "z": self.z}[axis]

    def at(self, axis, step):
        return lax.rem(self.pos(axis) + (step + 4), 4)

    def dev(self, axis, step):
        x, y, z, c = self.x, self.y, self.z, self.c
        if axis == "x":
            x = self.at("x", step)
        elif axis == "y":
            y = self.at("y", step)
        elif axis == "z":
            z = self.at("z", step)
        else:
            c = 1 - c
        return {"fsdp": y, "ctx": z * 8 + x * 2 + c}

    def copy(self, src, dst, axis, step=1):
        k = self.used
        self.used += 1
        cp = pltpu.make_async_remote_copy(
            src_ref=src,
            dst_ref=dst,
            send_sem=self.send_sem.at[k],
            recv_sem=self.recv_sem.at[k],
            device_id=self.dev(axis, step),
            device_id_type=MESH,
        )
        cp.start()
        self.sent.append(cp)
        return cp

    def barrier(self):
        sem = pltpu.get_barrier_semaphore()
        peers = [("c", 1), *[(a, s) for a in "xyz" for s in STEPS]]
        for axis, step in peers:
            pl.semaphore_signal(sem, inc=1, device_id=self.dev(axis, step), device_id_type=MESH)
        pl.semaphore_wait(sem, len(peers))

    def drain(self):
        for cp in self.sent:
            cp.wait_send()


class Relay:
    def __init__(self, net, axis, piece, own):
        self.net, self.axis, self.piece, self.own = net, axis, piece, own

    def start(self):
        self.up = [self.net.copy(a, b, self.axis, 1) for a, b in self.own]
        self.down = [self.net.copy(a, b, self.axis, -1) for a, b in self.own]

    def mid(self):
        for cp in self.up:
            cp.wait_recv()
        low = self.piece(self.net.at(self.axis, -1), 0)
        self.up2 = self.net.copy(low, low, self.axis, 1)
        for cp in self.down:
            cp.wait_recv()
        high = self.piece(self.net.at(self.axis, 1), 1)
        self.down2 = self.net.copy(high, high, self.axis, -1)

    def end(self):
        self.up2.wait_recv()
        self.down2.wait_recv()


class Gather:
    def __init__(self, net, axis, piece):
        self.net, self.axis, self.piece = net, axis, piece

    def start(self):
        own = self.piece(self.net.pos(self.axis))
        self.copies = [(s, self.net.copy(own, own, self.axis, s)) for s in (1, -1, 2)]

    def end(self, then=None):
        for s, cp in self.copies:
            cp.wait_recv()
            if then is not None:
                then(self.net.at(self.axis, -s))


class RelayScatter:
    def __init__(self, net, axis, q, bufs):
        self.net, self.axis, self.q, self.bufs = net, axis, q, bufs
        self.n = bufs[0].shape[1] // 2

    def half(self, ref, h):
        return ref.at[:, pl.ds(h * self.n, self.n)]

    def start(self):
        far = self.q(self.net.at(self.axis, 2))
        first = self.bufs[0]
        self.cl = self.net.copy(self.half(far, 0), self.half(first, 0), self.axis, 1)
        self.ch = self.net.copy(self.half(far, 1), self.half(first, 1), self.axis, -1)

    def mid(self):
        up, down = self.q(self.net.at(self.axis, 1)), self.q(self.net.at(self.axis, -1))
        first = self.bufs[0]
        self.cl.wait_recv()
        add_rows(self.half(up, 0), (self.half(first, 0),))
        self.cp = self.net.copy(up, self.bufs[1], self.axis, 1)
        self.ch.wait_recv()
        add_rows(self.half(down, 1), (self.half(first, 1),))
        self.cm = self.net.copy(down, self.bufs[2], self.axis, -1)

    def end(self, out=None):
        self.cp.wait_recv()
        self.cm.wait_recv()
        add_rows(self.q(self.net.pos(self.axis)), self.bufs[1:], out)


class Scatter:
    def __init__(self, net, axis, q, bufs):
        self.net, self.axis, self.q, self.bufs = net, axis, q, bufs
        self.copies = []

    def send(self, s):
        buf = self.bufs[STEPS.index(s)]
        self.copies.append(self.net.copy(self.q(self.net.at(self.axis, s)), buf, self.axis, s))

    def start(self):
        for s in STEPS:
            self.send(s)

    def end(self, out=None):
        for cp in self.copies:
            cp.wait_recv()
        add_rows(self.q(self.net.pos(self.axis)), self.bufs, out)


def add_rows(dst, srcs, out=None):
    target = dst if out is None else out
    lead, rows = dst.shape[:-2], dst.shape[-2]
    step = next(n for n in (256, 192, 128, 96, 64, 48, 32, 16) if rows % n == 0)
    per = rows // step
    count = per
    for n in lead:
        count *= n

    def body(i, _):
        idx = []
        k = lax.div(i, per)
        for n in reversed(lead):
            idx.insert(0, lax.rem(k, n))
            k = lax.div(k, n)
        idx = (*idx, pl.ds(pl.multiple_of(lax.rem(i, per) * step, 16), step), slice(None))
        total = dst[idx].astype(F32)
        for s in srcs:
            total += s[idx].astype(F32)
        target[idx] = total.astype(target.dtype)
        return 0

    lax.fori_loop(0, count, body, 0)


def tdot(a, b):
    return lax.dot_general(a, b, (((0,), (0,)), ((), ())), preferred_element_type=F32)


def dot(a, b):
    return jnp.dot(a, b, preferred_element_type=F32)


def dot_back(a, b):
    return lax.dot_general(a, b, (((1,), (1,)), ((), ())), preferred_element_type=F32)


def rms(v):
    return lax.rsqrt(jnp.mean(v * v, axis=-1, keepdims=True) + EPS)


def norm_back(v, r, g, u):
    ug = u * g
    return r * ug - v * (r * r * r) * jnp.mean(ug * v, axis=-1, keepdims=True)


def gain_grad(v, r, u):
    return jnp.sum(u * v * r, axis=0, keepdims=True)


def rope(u, cos, sin):
    a, b = u[:, :128], u[:, 128:]
    return jnp.concatenate([a * cos - b * sin, b * cos + a * sin], axis=1)


def rope_back(w, cos, sin):
    a, b = w[:, :128], w[:, 128:]
    return jnp.concatenate([a * cos + b * sin, b * cos - a * sin], axis=1)


def causal(net, c_key):
    row = lax.broadcasted_iota(jnp.int32, (512, 512), 0)
    col = lax.broadcasted_iota(jnp.int32, (512, 512), 1)
    q_pos = (net.x * 2 + net.c) * 128 + (row & 127)
    k_pos = (col >> 7) * 256 + c_key * 128 + (col & 127)
    return k_pos <= q_pos


class Group:
    def __init__(self, net, g, full, parts, bufs, relay=False):
        self.relay = relay
        self.net, self.g, self.full, self.parts, self.bufs = net, g, full, parts, bufs
        self.place = [[0, 4, off, rows] for off, rows, _ in parts]
        self.phase = -1

    def q(self, p, axis):
        y0, yn, r0, rn = self.place[p]

        def share(j):
            if axis == "y":
                return self.g.at[pl.ds(j, 1), pl.ds(pl.multiple_of(r0, 16), rn)]
            return self.g.at[pl.ds(y0, yn), pl.ds(pl.multiple_of(r0 + j * (rn // 4), 16), rn // 4)]

        return share

    def scatter_start(self, phase):
        self.runs = []
        for p, (_, _, order) in enumerate(self.parts):
            k = (p * 3 + phase) * 3
            kind = RelayScatter if self.relay and phase == 0 else Scatter
            self.runs.append(kind(self.net, order[phase], self.q(p, order[phase]), self.bufs[k : k + 3]))
            self.runs[-1].start()

    def scatter_end(self, phase):
        for p, r in enumerate(self.runs):
            y0, yn, r0, rn = self.place[p]
            axis = self.parts[p][2][phase]
            if axis == "y":
                self.place[p] = [self.net.y, 1, r0, rn]
            else:
                self.place[p] = [y0, yn, r0 + self.net.pos(axis) * (rn // 4), rn // 4]
            _, _, r0, rn = self.place[p]
            r.end(self.full.at[pl.ds(self.net.c, 1), pl.ds(pl.multiple_of(r0, 16), rn)] if phase == 2 else None)

    def mid(self):
        for r in self.runs:
            r.mid()

    def gather_start(self, stage):
        self.runs = []
        for off, rows, order in self.parts:
            u = rows // 16
            major, minor = order.replace("y", "")

            def piece(j, u=u, off=off, major=major):
                if stage == 0:
                    return self.full.at[self.net.c, pl.ds(pl.multiple_of(off + self.net.pos(major) * 4 * u + j * u, 16), u)]
                return self.full.at[self.net.c, pl.ds(pl.multiple_of(off + j * 4 * u, 16), 4 * u)]

            self.runs.append(Gather(self.net, minor if stage == 0 else major, piece))
            self.runs[-1].start()

    def step(self):
        done, self.phase = self.phase, self.phase + 1
        if 0 <= done < 3:
            self.scatter_end(done)
        elif 3 <= done < 5:
            for r in self.runs:
                r.end()
        elif done == 5:
            self.swap.wait_recv()
        if done < 2:
            self.scatter_start(done + 1)
        elif done < 4:
            self.gather_start(done - 2)
        elif done == 4:
            ref = self.full.at[self.net.c, pl.ds(self.parts[0][0], sum(rows for _, rows, _ in self.parts))]
            self.swap = self.net.copy(ref, ref, "c")


def group_bufs(parts):
    bufs = []
    for _, rows, order in parts:
        lead = 4
        for axis in order:
            if axis == "y":
                lead = 1
            else:
                rows //= 4
            bufs += [VMEM((lead, rows, 128), BF)] * 3
    return bufs


ALL_PARTS = (EA_PARTS, EB_PARTS, M_PARTS, L_PARTS)


def layer_kernel(*refs):
    refs = list(refs)

    def take_refs(n):
        out = refs[:n]
        del refs[:n]
        return out

    wq, wk, wv, wo, wg, wu, wd = take_refs(7)
    gain_ins = take_refs(6)
    tokens, cot, cos, sin = take_refs(4)
    layer_out, input_grad, e_full, m_full, l_full = take_refs(5)
    qkv_all, gu, wo_all, wd_all, k_all, v_all = take_refs(6)
    normed, qkvg, attn, projg, ffn, gug, mixed, downg = take_refs(8)
    gain_all, gains, gain_s, gain_other, ge, gm, gl = take_refs(7)
    dk, dv, kin, vin, acc, inv_s, delta_s, do_s, q_s, raw, f_s, g_s, hidden_grad_s = take_refs(13)
    kbufs, vbufs, k2bufs, v2bufs = take_refs(3), take_refs(3), take_refs(3), take_refs(3)
    group_b = [take_refs(9 * len(parts)) for parts in ALL_PARTS]
    send_sem, recv_sem, own_sem = take_refs(3)
    net = Net(send_sem, recv_sem)
    y, c, x, z = net.y, net.c, net.x, net.z
    other = 1 - c
    own_rows, other_rows = pl.ds(0, 128), pl.ds(128, 128)
    own = []
    for k, (src, dst) in enumerate(
        [
            (wg, gu.at[y, :, pl.ds(0, 2048)]), (wu, gu.at[y, :, pl.ds(2048, 2048)]),
            (wq, qkv_all.at[y, :, pl.ds(0, 1024)]), (wk, qkv_all.at[y, :, pl.ds(1024, 256)]),
            (wv, qkv_all.at[y, :, pl.ds(1280, 256)]), (wo, wo_all.at[y]), (wd, wd_all.at[y]),
        ]
    ):
        own.append(pltpu.make_async_copy(src, dst, own_sem.at[k]))
        own[-1].start()
    gain_all[y] = jnp.zeros((8, 256), F32)
    for i, n in enumerate(GAIN_SIZES):
        gain_all[y, pl.ds(i, 1), pl.ds(0, n)] = gain_ins[i][...].astype(F32).reshape(1, n)
    net.barrier()
    for cp in own:
        cp.wait()

    rows = pl.ds(pl.multiple_of(c * 80, 16), 80)

    def block(yq, start, n):
        return gu.at[yq, rows, pl.ds(pl.multiple_of(start, 128), n)]

    def gate_one(yq, xj, zj):
        return block(yq, (zj * 4 + xj) * 128, 128)

    def up_one(yq, xj, zj):
        return block(yq, 2048 + (xj * 4 + zj) * 128, 128)

    def qkv_piece(yq, half=None):
        off, n = {None: (0, 1536), 0: (0, 768), 1: (768, 768)}[half]
        return qkv_all.at[yq, rows, pl.ds(off, n)]

    def gu_piece(yq):
        return gu.at[yq, rows]

    def row_piece(ref, size):
        def piece(yq, half=None):
            off, n = {None: (0, size), 0: (0, size // 2), 1: (size // 2, size // 2)}[half]
            return ref.at[yq, pl.ds(pl.multiple_of(c * size + off, 16), n)]

        return piece

    wo_piece, wd_piece = row_piece(wo_all, 128), row_piece(wd_all, 256)
    gu_y = [Gather(net, "y", lambda j: gate_one(j, x, z)), Gather(net, "y", lambda j: up_one(j, x, z))]
    for g in gu_y:
        g.start()
    qkv = Relay(net, "y", qkv_piece, [(qkv_piece(y), qkv_piece(y))])
    w_o = Relay(net, "y", wo_piece, [(wo_piece(y), wo_piece(y))])
    w_d = Relay(net, "y", wd_piece, [(wd_piece(y), wd_piece(y))])
    qkv.start()
    gain_own = gain_all.at[y]
    gain_copies = [net.copy(gain_own, gain_own, "y", s) for s in STEPS]
    for g in gu_y:
        g.end()
    gu_1, gu_2 = [], []
    for s in (1, -1, 2):
        yq = net.at("y", s)
        gu_1.append(Gather(net, "x", lambda j, yq=yq: gate_one(yq, j, z)))
        gu_1.append(Gather(net, "z", lambda j, yq=yq: up_one(yq, x, j)))
        gu_2.append(Gather(net, "z", lambda j, yq=yq: block(yq, j * 512, 512)))
        gu_2.append(Gather(net, "x", lambda j, yq=yq: block(yq, 2048 + j * 512, 512)))
    for g in gu_1:
        g.start()
    for cp in gain_copies:
        cp.wait_recv()
    all_gains = gain_all[...]

    def gain(i, n):
        return jnp.concatenate([all_gains[yq, i : i + 1, :n] for yq in range(4)], axis=1)

    gains[0:1, :] = gain(0, 160)
    for i in range(3, 6):
        gains[i : i + 1, :] = gain(i, 160)
    gains[1:2, 0:256] = gain(1, 64)
    gains[2:3, 0:256] = gain(2, 64)
    g_in, g_q, g_k = gains[0:1, :], gains[1:2, 0:256], gains[2:3, 0:256]
    g_post, g_pre, g_fpost = gains[3:4, :], gains[4:5, :], gains[5:6, :]
    t = tokens[...].astype(F32)
    normed_low = (t * rms(t) * g_in).astype(BF)
    normed[own_rows, :] = normed_low

    def share(ref):
        return net.copy(ref.at[own_rows], ref.at[other_rows], "c")

    swaps = {}

    def swap(name, piece, j):
        swaps.setdefault(name, []).append(net.copy(piece(j), piece(j), "c"))

    def swapped(name):
        for cp in swaps[name]:
            cp.wait_recv()

    qkv.mid()
    w_o.start()
    w_d.start()
    swap("qkv", qkv_piece, net.at("y", 1))
    swap("qkv", qkv_piece, net.at("y", -1))
    for a, b in zip(gu_1, gu_2):
        a.end()
    for b in gu_2:
        b.start()
    qkv.end()
    swap("qkv", qkv_piece, net.at("y", 2))
    swapped("qkv")
    both = dot(normed_low, qkv_all[:, :, pl.ds(1024, 512)].reshape(640, 512))
    u = both[:, 0:256]
    raw[:, pl.ds(1024, 256)] = u
    k_all[c, z, x] = rope(u * rms(u) * g_k, cos[...], sin[...]).astype(BF)
    v_all[c, z, x] = both[:, 256:512].astype(BF)
    kx = Gather(net, "x", lambda j: k_all.at[c, z, j])
    vz = Gather(net, "z", lambda j: v_all.at[c, j, x])
    kz = Gather(net, "z", lambda j: k_all.at[c, j])
    vx = Gather(net, "x", lambda j: v_all.at[c, :, j])
    kx.start()
    vz.start()
    both = dot(normed_low, qkv_all[:, :, pl.ds(0, 1024)].reshape(640, 1024))
    raw[:, pl.ds(0, 1024)] = both
    for h in range(4):
        u = both[:, h * 256 : h * 256 + 256]
        q_s[pl.ds(h * 128, 128), :] = (rope(u * rms(u) * g_q, cos[...], sin[...]).astype(BF) * 0.0625).astype(BF)

    def swap_k(j):
        swap("kv", lambda j: k_all.at[c, j], j)

    def swap_v(j):
        swap("kv", lambda j: v_all.at[c, :, j], j)

    kx.end()
    kz.start()
    vz.end()
    vx.start()
    swap_k(z)
    swap_v(x)
    acc[...] = jnp.zeros_like(acc)
    inv_s[...] = jnp.zeros_like(inv_s)
    gain_s[...] = jnp.zeros_like(gain_s)
    ge[:, pl.ds(E_END, E_ROWS - E_END), :] = jnp.zeros((4, E_ROWS - E_END, 128), BF)
    gm[:, pl.ds(M_END, M_ROWS - M_END), :] = jnp.zeros((4, M_ROWS - M_END, 128), BF)
    gl[:, pl.ds(L_END, L_ROWS - L_END), :] = jnp.zeros((4, L_ROWS - L_END, 128), BF)
    shared = {"normed": share(normed)}
    w_o.mid()
    w_d.mid()
    for name, piece in (("wo", wo_piece), ("wd", wd_piece)):
        swap(name, piece, net.at("y", 1))
        swap(name, piece, net.at("y", -1))
    for g in gu_2:
        g.end()
    for s in (1, -1, 2):
        swap("gu", gu_piece, net.at("y", s))
    kz.end(swap_k)
    vx.end(swap_v)
    for r, name, piece in ((w_o, "wo", wo_piece), (w_d, "wd", wd_piece)):
        r.end()
        swap(name, piece, net.at("y", 2))
    swapped("kv")

    def fwd_tile(cc, j, diagonal):
        p = jnp.exp(dot_back(q_s[...], k_all[cc, j].reshape(512, 256)))
        if diagonal:
            p = jnp.where(causal(net, cc), p, 0.0)
        inv_s[...] += jnp.sum(p, axis=1, keepdims=True)
        acc[...] += dot(p.astype(BF), v_all[cc, j].reshape(512, 256))

    def fwd_step(i, _):
        fwd_tile(lax.rem(i, 2), lax.div(i, 2), False)
        return 0

    def fwd_last(i, _):
        fwd_tile(i, z, True)
        return 0

    lax.fori_loop(0, z * 2, fwd_step, 0)
    lax.fori_loop(0, 2, fwd_last, 0)
    inv = 1.0 / inv_s[...]
    inv_s[...] = inv
    acc[...] = acc[...] * inv
    for h in range(4):
        attn[own_rows, pl.ds(h * 256, 256)] = acc[pl.ds(h * 128, 128), :].astype(BF)
    shared["attn"] = share(attn)

    def put_gain(i, value):
        n = value.shape[1] // 4
        for yq in range(4):
            v = value[:, yq * n : yq * n + n]
            gain_s[yq, pl.ds(2 * i, 1), pl.ds(0, min(n, 128))] = v[:, :128]
            if n > 128:
                gain_s[yq, pl.ds(2 * i + 1, 1), pl.ds(0, n - 128)] = v[:, 128:]

    swapped("wo")
    w_out = wo_all[...].reshape(1024, 640)
    proj = dot(attn[own_rows, :], w_out)
    r_proj = rms(proj)
    hidden = tokens[...].astype(F32) + proj * r_proj * g_post
    r_hidden = rms(hidden)
    ffn_low = (hidden * r_hidden * g_pre).astype(BF)
    ffn[own_rows, :] = ffn_low
    shared["ffn"] = share(ffn)
    swapped("gu")
    for i in range(4):
        cs, cs2 = pl.ds(i * 512, 512), pl.ds(2048 + i * 512, 512)
        gate = dot(ffn_low, gu[:, :, cs].reshape(640, 512))
        up = dot(ffn_low, gu[:, :, cs2].reshape(640, 512))
        t = jnp.tanh(C_ROOT * (gate + C_CUBE * gate * gate * gate))
        gelu = 0.5 * gate * (1.0 + t)
        slope = 0.5 * (1.0 + t) + 0.5 * gate * (1.0 - t * t) * (C_ROOT * (1.0 + 3.0 * C_CUBE * gate * gate))
        mixed[own_rows, cs] = (gelu * up).astype(BF)
        f_s[:, cs] = up * slope
        g_s[:, cs] = gelu
    shared["mixed"] = share(mixed)
    swapped("wd")
    down = dot(mixed[own_rows, :], wd_all[...].reshape(2048, 640))
    r_down = rms(down)
    layer_out[...] = (hidden + down * r_down * g_fpost).astype(BF)
    out_grad = cot[...].astype(F32)
    down_grad = norm_back(down, r_down, g_fpost, out_grad).astype(BF)
    put_gain(5, gain_grad(down, r_down, out_grad))
    downg[own_rows, :] = down_grad
    shared["downg"] = share(downg)
    for i in range(4):
        cs, cs2 = pl.ds(i * 512, 512), pl.ds(2048 + i * 512, 512)
        mg = dot_back(down_grad, wd_all[i])
        gug[own_rows, cs] = (mg * f_s[:, cs]).astype(BF)
        gug[own_rows, cs2] = (mg * g_s[:, cs]).astype(BF)
    shared["gug"] = share(gug)
    ffn_grad = dot_back(gug[own_rows, :], gu[...].reshape(640, 4096))
    hidden_grad = out_grad + norm_back(hidden, r_hidden, g_pre, ffn_grad)
    put_gain(4, gain_grad(hidden, r_hidden, ffn_grad))
    hidden_grad_s[...] = hidden_grad
    proj_grad = norm_back(proj, r_proj, g_post, hidden_grad).astype(BF)
    put_gain(3, gain_grad(proj, r_proj, hidden_grad))
    projg[own_rows, :] = proj_grad
    shared["projg"] = share(projg)
    def cols(start, width):
        return pl.ds(pl.multiple_of(start, 128), width)

    def put(g, off, n, value, col_blocks):
        value = value.astype(BF)
        for yq in range(4):
            for j in range(col_blocks):
                g[yq, pl.ds(off + j * n, n), :] = value[yq * n : yq * n + n, j * 128 : j * 128 + 128]

    for name in ("ffn", "gug"):
        shared[name].wait_recv()
    for part in range(2):
        put(ge, OFF_G + part * 640, 160, tdot(ffn[...], gug[:, cols(c * 1024 + part * 512, 512)]), 4)
        put(ge, OFF_U + part * 640, 160, tdot(ffn[...], gug[:, cols(2048 + c * 1024 + part * 512, 512)]), 4)
    early_a = Group(net, ge, e_full, EA_PARTS, group_b[0], relay=True)
    early_a.step()
    attn_grad = dot_back(proj_grad, w_out).astype(BF)
    for h in range(4):
        do_s[pl.ds(h * 128, 128), :] = attn_grad[:, h * 256 : h * 256 + 256]
    delta_s[...] = jnp.sum(do_s[...].astype(F32) * acc[...], axis=1, keepdims=True)

    for name in ("attn", "mixed", "downg", "projg"):
        shared[name].wait_recv()
    for yq in range(4):
        value = tdot(attn[:, cols(yq * 256 + c * 128, 128)], projg[...]).astype(BF)
        for j in range(5):
            ge[yq, pl.ds(OFF_O + j * 128, 128), :] = value[:, j * 128 : j * 128 + 128]
        value = tdot(mixed[:, cols(yq * 512 + c * 256, 256)], downg[...]).astype(BF)
        for j in range(5):
            ge[yq, pl.ds(OFF_D + j * 256, 256), :] = value[:, j * 128 : j * 128 + 128]
    early_b = Group(net, ge, e_full, EB_PARTS, group_b[1])
    early_b.step()

    acc[...] = jnp.zeros_like(acc)

    def tile(cc, j, diagonal):
        kt, vt = k_all[cc, j].reshape(512, 256), v_all[cc, j].reshape(512, 256)
        p = jnp.exp(dot_back(q_s[...], kt)) * inv_s[...]
        if diagonal:
            p = jnp.where(causal(net, cc), p, 0.0)
        ds = (p * (dot_back(do_s[...], vt) - delta_s[...])).astype(BF)
        acc[...] += dot(ds, kt)
        dk[cc, j] = tdot(ds, q_s[...]).astype(BF).reshape(4, 128, 256)
        dv[cc, j] = tdot(p.astype(BF), do_s[...]).astype(BF).reshape(4, 128, 256)

    kc, vc = {}, {}

    def tiles(s):
        j = net.at("z", s)

        def step(i, _):
            cc = lax.rem(other + i, 2)
            if s == 0:
                tile(cc, j, True)
            else:

                @pl.when(j < z)
                def _():
                    tile(cc, j, False)

                @pl.when(j > z)
                def _():
                    dk[cc, j] = jnp.zeros((4, 128, 256), BF)
                    dv[cc, j] = jnp.zeros((4, 128, 256), BF)

            return 0

        lax.fori_loop(0, 2, step, 0)
        kc[s] = net.copy(dk.at[other, j], kin.at[j], "c")
        vc[s] = net.copy(dv.at[other, j], vin.at[j], "c")

    k1 = Scatter(net, "z", lambda j: kin.at[j], kbufs)
    v1 = Scatter(net, "x", lambda j: vin.at[:, j], vbufs)
    k2 = Scatter(net, "x", lambda j: kin.at[z, j], k2bufs)
    v2 = Scatter(net, "z", lambda j: vin.at[j, x], v2bufs)

    def take(s):
        j = net.at("z", s)
        kc[s].wait_recv()
        add_rows(kin.at[j], (dk.at[c, j],))
        if s != 0:
            k1.send(s)
        vc[s].wait_recv()
        add_rows(vin.at[j], (dv.at[c, j],))

    tiles(2)
    tiles(1)
    take(2)
    tiles(-1)
    take(1)
    early_a.mid()
    tiles(0)
    take(-1)
    take(0)
    v1.start()

    total_q = jnp.zeros((1, 256), F32)
    for h in range(4):
        v = raw[:, pl.ds(h * 256, 256)]
        r = rms(v)
        u = rope_back(acc[pl.ds(h * 128, 128), :] * 0.0625, cos[...], sin[...])
        total_q += gain_grad(v, r, u)
        qkvg[own_rows, pl.ds(h * 256, 256)] = norm_back(v, r, g_q, u).astype(BF)
    put_gain(1, total_q)
    q_cols, kv_cols = pl.ds(0, 1024), pl.ds(1024, 512)
    share_q = net.copy(qkvg.at[own_rows, q_cols], qkvg.at[other_rows, q_cols], "c")
    normed_grad = dot_back(qkvg[own_rows, q_cols], qkv_all[:, :, q_cols].reshape(640, 1024))
    early_b.step()
    shared["normed"].wait_recv()
    share_q.wait_recv()
    put(gm, OFF_Q, 160, tdot(normed[...], qkvg[:, cols(c * 512, 512)]), 4)
    middle = Group(net, gm, m_full, M_PARTS, group_b[2])
    k1.end()
    k2.start()
    v1.end()
    v2.start()
    middle.step()
    early_b.step()
    k2.end()
    v2.end()
    early_a.step()

    v = raw[:, pl.ds(1024, 256)]
    r = rms(v)
    u = rope_back(kin[z, x].astype(F32), cos[...], sin[...])
    put_gain(2, gain_grad(v, r, u))
    qkvg[own_rows, pl.ds(1024, 256)] = norm_back(v, r, g_k, u).astype(BF)
    qkvg[own_rows, pl.ds(1280, 256)] = vin[z, x]
    share_kv = net.copy(qkvg.at[own_rows, kv_cols], qkvg.at[other_rows, kv_cols], "c")
    normed_grad = normed_grad + dot_back(qkvg[own_rows, kv_cols], qkv_all[:, :, kv_cols].reshape(640, 512))
    t = tokens[...].astype(F32)
    r = rms(t)
    put_gain(0, gain_grad(t, r, normed_grad))
    gain_copy = net.copy(gain_s, gain_other, "c")
    input_grad[...] = hidden_grad_s[...] + norm_back(t, r, g_in, normed_grad)
    middle.step()
    share_kv.wait_recv()
    put(gl, OFF_K, 160, tdot(normed[...], qkvg[:, cols(1024 + c * 128, 128)]), 1)
    put(gl, OFF_V, 160, tdot(normed[...], qkvg[:, cols(1280 + c * 128, 128)]), 1)
    gain_copy.wait_recv()
    gl[:, pl.ds(OFF_GAIN, 16), :] = (gain_s[...] + gain_other[...]).astype(BF)
    late = Group(net, gl, l_full, L_PARTS, group_b[3])
    late.step()
    early_a.step()
    early_b.step()
    middle.step()
    late.step()
    early_a.step()
    early_b.step()
    middle.step()
    late.step()
    early_a.step()
    early_b.step()
    middle.step()
    late.step()
    early_a.step()
    middle.step()
    late.step()
    early_a.step()
    late.step()
    early_b.step()
    middle.step()
    late.step()
    net.drain()


def layer(*args):
    def s(dtype, *shape):
        return jax.ShapeDtypeStruct(shape, dtype)

    n = 6 + 4 + 3 + 18 + 18 + 3 + 4 + 4 + 3 + 3 + 3 + 12 + 8 + 8 + 2 + 8 + 12 + sum(16 * len(p) + 1 for p in ALL_PARTS)
    big, small = VMEM((4, 128, 256), BF), VMEM((128, 256), BF)
    whole = VMEM((2, 4, 4, 128, 256), BF)
    column = VMEM((512, 1), F32)
    return pl.pallas_call(
        layer_kernel,
        out_shape=(
            s(BF, 128, 640), s(F32, 128, 640), s(BF, 2, E_ROWS, 128), s(BF, 2, M_ROWS, 128), s(BF, 2, L_ROWS, 128)
        ),
        in_specs=[ANYSPEC] * 7 + [VSPEC] * 10,
        out_specs=[VSPEC] * 5,
        scratch_shapes=[
            VMEM((4, 160, 1536), BF), VMEM((4, 160, 4096), BF), VMEM((4, 256, 640), BF), VMEM((4, 512, 640), BF),
            whole, whole,
            *[VMEM((256, n), BF) for n in (640, 1536, 1024, 640, 640, 4096, 2048, 640)],
            VMEM((4, 8, 256), F32), VMEM((8, 640), F32), VMEM((4, 16, 128), F32), VMEM((4, 16, 128), F32),
            VMEM((4, E_ROWS, 128), BF), VMEM((4, M_ROWS, 128), BF), VMEM((4, L_ROWS, 128), BF),
            whole, whole, VMEM((4, 4, 128, 256), BF), VMEM((4, 4, 128, 256), BF),
            VMEM((512, 256), F32), column, column, VMEM((512, 256), BF), VMEM((512, 256), BF), VMEM((128, 1280), F32),
            VMEM((128, 2048), F32), VMEM((128, 2048), F32), VMEM((128, 640), F32),
            *[big] * 6, *[small] * 6,
            *[b for parts in ALL_PARTS for b in group_bufs(parts)],
            pltpu.SemaphoreType.DMA((n,)),
            pltpu.SemaphoreType.DMA((n,)),
            pltpu.SemaphoreType.DMA((7,)),
        ],
        compiler_params=pltpu.CompilerParams(collective_id=0, has_side_effects=True, vmem_limit_bytes=VMEM_LIMIT),
        name="layer",
    )(*args)


def unpack_kernel(e, m, l, lo, ig, lo_out, ig_out, oq, ok, ov, oo, og, ou, od, *gain_outs):
    lo_out[...] = lo[...]
    ig_out[...] = ig[...]
    for c in range(2):

        def block(full, off, n, j):
            return full[c, pl.ds(off + j * n, n), :].astype(F32)

        for j in range(4):
            oq[:, pl.ds(c * 512 + j * 128, 128)] = block(m, OFF_Q, 160, j)
        ok[:, pl.ds(c * 128, 128)] = block(l, OFF_K, 160, 0)
        ov[:, pl.ds(c * 128, 128)] = block(l, OFF_V, 160, 0)
        for j in range(8):
            og[:, pl.ds(c * 1024 + j * 128, 128)] = block(e, OFF_G, 160, j)
            ou[:, pl.ds(c * 1024 + j * 128, 128)] = block(e, OFF_U, 160, j)
        for j in range(5):
            oo[pl.ds(c * 128, 128), pl.ds(j * 128, 128)] = block(e, OFF_O, 128, j)
            od[pl.ds(c * 256, 256), pl.ds(j * 128, 128)] = block(e, OFF_D, 256, j)
    rows = l[0, pl.ds(OFF_GAIN, 16), :].astype(F32)
    for i, n in enumerate(GAIN_SIZES):
        gain_outs[i][:, pl.ds(0, min(n, 128))] = rows[2 * i : 2 * i + 1, : min(n, 128)]
        if n > 128:
            gain_outs[i][:, pl.ds(128, n - 128)] = rows[2 * i + 1 : 2 * i + 2, : n - 128]


def unpack(e, m, l, lo, ig):
    def s(*shape):
        return jax.ShapeDtypeStruct(shape, F32)

    return pl.pallas_call(
        unpack_kernel,
        out_shape=(
            jax.ShapeDtypeStruct((128, 640), BF), s(128, 640), s(160, 1024), s(160, 256), s(160, 256), s(256, 640), s(160, 2048), s(160, 2048), s(512, 640),
            *[s(1, n) for n in GAIN_SIZES],
        ),
        in_specs=[VSPEC] * 5,
        out_specs=[VSPEC] * 15,
        compiler_params=pltpu.CompilerParams(vmem_limit_bytes=VMEM_LIMIT),
        name="unpack",
    )(e, m, l, lo, ig)


def local(
    tokens, positions, w_query, w_key, w_value, w_out, w_gate, w_up, w_down,
    gain_in, gain_query, gain_key, gain_attn_post, gain_ffn_pre, gain_ffn_post, cotangent,
):
    gains = (gain_in, gain_query, gain_key, gain_attn_post, gain_ffn_pre, gain_ffn_post)
    exponents = jnp.arange(0, 256, 2, dtype=F32) / 256
    inverse = 1.0 / ROPE_BASE**exponents
    angles = positions.astype(F32)[:, None] * inverse[None, :]
    cos, sin = jnp.cos(angles), jnp.sin(angles)
    layer_out, input_grad, e_full, m_full, l_full = layer(
        w_query, w_key, w_value, w_out, w_gate, w_up, w_down, *gains, tokens, cotangent, cos, sin
    )
    layer_out, input_grad, oq, ok, ov, oo, og, ou, od, *gain_grads = unpack(e_full, m_full, l_full, layer_out, input_grad)
    return (layer_out, input_grad, oq, ok, ov, oo, og, ou, od, *[g.reshape(g.shape[1]) for g in gain_grads])


def solution(mesh):
    rows, both, vec = P("fsdp", None), P(("fsdp", "ctx"), None), P("fsdp")
    in_specs = (both, P(("fsdp", "ctx")), *[rows] * 7, *[vec] * 6, both)
    out_specs = (both, both, *[rows] * 7, *[vec] * 6)
    return jax.shard_map(local, mesh=mesh, in_specs=in_specs, out_specs=out_specs, check_vma=False)
```

```python
import functools

import jax
import jax.numpy as jnp
from jax import lax
from jax.experimental import pallas as pl
from jax.experimental.pallas import tpu as pltpu
from jax.sharding import PartitionSpec as P

EPS = 1e-06
ROPE_BASE = 1000000.0
BF = jnp.bfloat16
F32 = jnp.float32
MESH = pl.DeviceIdType.MESH
VMEM = pltpu.VMEM
VSPEC = pl.BlockSpec(memory_space=pltpu.VMEM)
ANYSPEC = pl.BlockSpec(memory_space=pl.ANY)
VMEM_LIMIT = 60 * 1024 * 1024
C_ROOT = 0.7978845608028654
C_CUBE = 0.044715

E_ROWS, M_ROWS, L_ROWS = 4608, 768, 512
OFF_G, OFF_U, OFF_O, OFF_D, E_END = 0, 1280, 2560, 3200, 4480
OFF_Q, M_END = 0, 640
OFF_K, OFF_V, OFF_GAIN, L_END = 0, 160, 320, 336
EA_PARTS = ((0, 1280, "yzx"), (1280, 1280, "yxz"))
EB_PARTS = ((2560, 1024, "xzy"), (3584, 1024, "zxy"))
M_PARTS = ((0, 256, "yzx"), (256, 256, "xzy"), (512, 256, "zxy"))
L_PARTS = ((0, 256, "yzx"), (256, 256, "xyz"))
GAIN_SIZES = (160, 64, 64, 160, 160, 160)
STEPS = (2, 1, -1)


class Net:
    def __init__(self, send_sem, recv_sem):
        me = lax.axis_index("ctx")
        self.y = lax.axis_index("fsdp")
        self.c = lax.rem(me, 2)
        self.x = lax.rem(lax.div(me, 2), 4)
        self.z = lax.div(me, 8)
        self.send_sem, self.recv_sem = send_sem, recv_sem
        self.used = 0
        self.sent = []

    def pos(self, axis):
        return {"x": self.x, "y": self.y, "z": self.z}[axis]

    def at(self, axis, step):
        return lax.rem(self.pos(axis) + (step + 4), 4)

    def dev(self, axis, step):
        x, y, z, c = self.x, self.y, self.z, self.c
        if axis == "x":
            x = self.at("x", step)
        elif axis == "y":
            y = self.at("y", step)
        elif axis == "z":
            z = self.at("z", step)
        else:
            c = 1 - c
        return {"fsdp": y, "ctx": z * 8 + x * 2 + c}

    def copy(self, src, dst, axis, step=1):
        k = self.used
        self.used += 1
        cp = pltpu.make_async_remote_copy(
            src_ref=src,
            dst_ref=dst,
            send_sem=self.send_sem.at[k],
            recv_sem=self.recv_sem.at[k],
            device_id=self.dev(axis, step),
            device_id_type=MESH,
        )
        cp.start()
        self.sent.append(cp)
        return cp

    def barrier(self):
        sem = pltpu.get_barrier_semaphore()
        peers = [("c", 1), *[(a, s) for a in "xyz" for s in STEPS]]
        for axis, step in peers:
            pl.semaphore_signal(sem, inc=1, device_id=self.dev(axis, step), device_id_type=MESH)
        pl.semaphore_wait(sem, len(peers))

    def drain(self):
        for cp in self.sent:
            cp.wait_send()


class Relay:
    def __init__(self, net, axis, piece, own):
        self.net, self.axis, self.piece, self.own = net, axis, piece, own

    def start(self):
        self.up = [self.net.copy(a, b, self.axis, 1) for a, b in self.own]
        self.down = [self.net.copy(a, b, self.axis, -1) for a, b in self.own]

    def mid(self):
        for cp in self.up:
            cp.wait_recv()
        low = self.piece(self.net.at(self.axis, -1), 0)
        self.up2 = self.net.copy(low, low, self.axis, 1)
        for cp in self.down:
            cp.wait_recv()
        high = self.piece(self.net.at(self.axis, 1), 1)
        self.down2 = self.net.copy(high, high, self.axis, -1)

    def end(self):
        self.up2.wait_recv()
        self.down2.wait_recv()


class Gather:
    def __init__(self, net, axis, piece):
        self.net, self.axis, self.piece = net, axis, piece

    def start(self):
        own = self.piece(self.net.pos(self.axis))
        self.copies = [(s, self.net.copy(own, own, self.axis, s)) for s in (1, -1, 2)]

    def end(self, then=None):
        for s, cp in self.copies:
            cp.wait_recv()
            if then is not None:
                then(self.net.at(self.axis, -s))


class RelayScatter:
    def __init__(self, net, axis, q, bufs):
        self.net, self.axis, self.q, self.bufs = net, axis, q, bufs
        self.n = bufs[0].shape[1] // 2

    def half(self, ref, h):
        return ref.at[:, pl.ds(h * self.n, self.n)]

    def start(self):
        far = self.q(self.net.at(self.axis, 2))
        first = self.bufs[0]
        self.cl = self.net.copy(self.half(far, 0), self.half(first, 0), self.axis, 1)
        self.ch = self.net.copy(self.half(far, 1), self.half(first, 1), self.axis, -1)

    def mid(self):
        up, down = self.q(self.net.at(self.axis, 1)), self.q(self.net.at(self.axis, -1))
        first = self.bufs[0]
        self.cl.wait_recv()
        add_rows(self.half(up, 0), (self.half(first, 0),))
        self.cp = self.net.copy(up, self.bufs[1], self.axis, 1)
        self.ch.wait_recv()
        add_rows(self.half(down, 1), (self.half(first, 1),))
        self.cm = self.net.copy(down, self.bufs[2], self.axis, -1)

    def end(self, out=None):
        self.cp.wait_recv()
        self.cm.wait_recv()
        add_rows(self.q(self.net.pos(self.axis)), self.bufs[1:], out)


class Scatter:
    def __init__(self, net, axis, q, bufs):
        self.net, self.axis, self.q, self.bufs = net, axis, q, bufs
        self.copies = []

    def send(self, s):
        buf = self.bufs[STEPS.index(s)]
        self.copies.append(self.net.copy(self.q(self.net.at(self.axis, s)), buf, self.axis, s))

    def start(self):
        for s in STEPS:
            self.send(s)

    def end(self, out=None):
        for cp in self.copies:
            cp.wait_recv()
        add_rows(self.q(self.net.pos(self.axis)), self.bufs, out)


def add_rows(dst, srcs, out=None):
    target = dst if out is None else out
    lead, rows = dst.shape[:-2], dst.shape[-2]
    step = next(n for n in (256, 192, 128, 96, 64, 48, 32, 16) if rows % n == 0)
    per = rows // step
    count = per
    for n in lead:
        count *= n

    def body(i, _):
        idx = []
        k = lax.div(i, per)
        for n in reversed(lead):
            idx.insert(0, lax.rem(k, n))
            k = lax.div(k, n)
        idx = (*idx, pl.ds(pl.multiple_of(lax.rem(i, per) * step, 16), step), slice(None))
        total = dst[idx].astype(F32)
        for s in srcs:
            total += s[idx].astype(F32)
        target[idx] = total.astype(target.dtype)
        return 0

    lax.fori_loop(0, count, body, 0)


def tdot(a, b):
    return lax.dot_general(a, b, (((0,), (0,)), ((), ())), preferred_element_type=F32)


def dot(a, b):
    return jnp.dot(a, b, preferred_element_type=F32)


def dot_back(a, b):
    return lax.dot_general(a, b, (((1,), (1,)), ((), ())), preferred_element_type=F32)


def rms(v):
    return lax.rsqrt(jnp.mean(v * v, axis=-1, keepdims=True) + EPS)


def norm_back(v, r, g, u):
    ug = u * g
    return r * ug - v * (r * r * r) * jnp.mean(ug * v, axis=-1, keepdims=True)


def gain_grad(v, r, u):
    return jnp.sum(u * v * r, axis=0, keepdims=True)


def rope(u, cos, sin):
    a, b = u[:, :128], u[:, 128:]
    return jnp.concatenate([a * cos - b * sin, b * cos + a * sin], axis=1)


def rope_back(w, cos, sin):
    a, b = w[:, :128], w[:, 128:]
    return jnp.concatenate([a * cos + b * sin, b * cos - a * sin], axis=1)


def causal(net, c_key):
    row = lax.broadcasted_iota(jnp.int32, (512, 512), 0)
    col = lax.broadcasted_iota(jnp.int32, (512, 512), 1)
    q_pos = (net.x * 2 + net.c) * 128 + (row & 127)
    k_pos = (col >> 7) * 256 + c_key * 128 + (col & 127)
    return k_pos <= q_pos


class Group:
    def __init__(self, net, g, full, parts, bufs, relay=False):
        self.relay = relay
        self.net, self.g, self.full, self.parts, self.bufs = net, g, full, parts, bufs
        self.place = [[0, 4, off, rows] for off, rows, _ in parts]
        self.phase = -1

    def q(self, p, axis):
        y0, yn, r0, rn = self.place[p]

        def share(j):
            if axis == "y":
                return self.g.at[pl.ds(j, 1), pl.ds(pl.multiple_of(r0, 16), rn)]
            return self.g.at[pl.ds(y0, yn), pl.ds(pl.multiple_of(r0 + j * (rn // 4), 16), rn // 4)]

        return share

    def scatter_start(self, phase):
        self.runs = []
        for p, (_, _, order) in enumerate(self.parts):
            k = (p * 3 + phase) * 3
            kind = RelayScatter if self.relay and phase == 0 else Scatter
            self.runs.append(kind(self.net, order[phase], self.q(p, order[phase]), self.bufs[k : k + 3]))
            self.runs[-1].start()

    def scatter_end(self, phase):
        for p, r in enumerate(self.runs):
            y0, yn, r0, rn = self.place[p]
            axis = self.parts[p][2][phase]
            if axis == "y":
                self.place[p] = [self.net.y, 1, r0, rn]
            else:
                self.place[p] = [y0, yn, r0 + self.net.pos(axis) * (rn // 4), rn // 4]
            _, _, r0, rn = self.place[p]
            r.end(self.full.at[pl.ds(self.net.c, 1), pl.ds(pl.multiple_of(r0, 16), rn)] if phase == 2 else None)

    def mid(self):
        for r in self.runs:
            r.mid()

    def gather_start(self, stage):
        self.runs = []
        for off, rows, order in self.parts:
            u = rows // 16
            major, minor = order.replace("y", "")

            def piece(j, u=u, off=off, major=major):
                if stage == 0:
                    return self.full.at[self.net.c, pl.ds(pl.multiple_of(off + self.net.pos(major) * 4 * u + j * u, 16), u)]
                return self.full.at[self.net.c, pl.ds(pl.multiple_of(off + j * 4 * u, 16), 4 * u)]

            self.runs.append(Gather(self.net, minor if stage == 0 else major, piece))
            self.runs[-1].start()

    def step(self):
        done, self.phase = self.phase, self.phase + 1
        if 0 <= done < 3:
            self.scatter_end(done)
        elif 3 <= done < 5:
            for r in self.runs:
                r.end()
        elif done == 5:
            self.swap.wait_recv()
        if done < 2:
            self.scatter_start(done + 1)
        elif done < 4:
            self.gather_start(done - 2)
        elif done == 4:
            ref = self.full.at[self.net.c, pl.ds(self.parts[0][0], sum(rows for _, rows, _ in self.parts))]
            self.swap = self.net.copy(ref, ref, "c")


def group_bufs(parts):
    bufs = []
    for _, rows, order in parts:
        lead = 4
        for axis in order:
            if axis == "y":
                lead = 1
            else:
                rows //= 4
            bufs += [VMEM((lead, rows, 128), BF)] * 3
    return bufs


ALL_PARTS = (EA_PARTS, EB_PARTS, M_PARTS, L_PARTS)


def layer_kernel(*refs):
    refs = list(refs)

    def take_refs(n):
        out = refs[:n]
        del refs[:n]
        return out

    wq, wk, wv, wo, wg, wu, wd = take_refs(7)
    gain_ins = take_refs(6)
    tokens, cot, positions, inverse = take_refs(4)
    layer_out, input_grad, e_out, m_out, l_full = take_refs(5)
    e_full, m_full = take_refs(2)
    qkv_all, gu, wo_all, wd_all, k_all, v_all = take_refs(6)
    normed, qkvg, attn, projg, ffn, gug, mixed, downg = take_refs(8)
    gain_all, gains, gain_s, gain_other, ge, gm, gl = take_refs(7)
    cos, sin = take_refs(2)
    dk, dv, kin, vin, acc, inv_s, delta_s, do_s, q_s, raw, f_s, g_s, hidden_grad_s = take_refs(13)
    kbufs, vbufs, k2bufs, v2bufs = take_refs(3), take_refs(3), take_refs(3), take_refs(3)
    group_b = [take_refs(9 * len(parts)) for parts in ALL_PARTS]
    send_sem, recv_sem, own_sem = take_refs(3)
    net = Net(send_sem, recv_sem)
    y, c, x, z = net.y, net.c, net.x, net.z
    other = 1 - c
    own_rows, other_rows = pl.ds(0, 128), pl.ds(128, 128)
    own = []
    for k, (src, dst) in enumerate(
        [
            (wg, gu.at[y, :, pl.ds(0, 2048)]), (wu, gu.at[y, :, pl.ds(2048, 2048)]),
            (wq, qkv_all.at[y, :, pl.ds(0, 1024)]), (wk, qkv_all.at[y, :, pl.ds(1024, 256)]),
            (wv, qkv_all.at[y, :, pl.ds(1280, 256)]), (wo, wo_all.at[y]), (wd, wd_all.at[y]),
        ]
    ):
        own.append(pltpu.make_async_copy(src, dst, own_sem.at[k]))
        own[-1].start()
    gain_all[y] = jnp.zeros((8, 256), F32)
    for i, n in enumerate(GAIN_SIZES):
        gain_all[y, pl.ds(i, 1), pl.ds(0, n)] = gain_ins[i][...].astype(F32).reshape(1, n)
    net.barrier()
    for cp in own:
        cp.wait()

    rows = pl.ds(pl.multiple_of(c * 80, 16), 80)

    def block(yq, start, n):
        return gu.at[yq, rows, pl.ds(pl.multiple_of(start, 128), n)]

    def gate_one(yq, xj, zj):
        return block(yq, (zj * 4 + xj) * 128, 128)

    def up_one(yq, xj, zj):
        return block(yq, 2048 + (xj * 4 + zj) * 128, 128)

    def qkv_piece(yq, half=None):
        off, n = {None: (0, 1536), 0: (0, 768), 1: (768, 768)}[half]
        return qkv_all.at[yq, rows, pl.ds(off, n)]

    def gu_piece(yq):
        return gu.at[yq, rows]

    def row_piece(ref, size):
        def piece(yq, half=None):
            off, n = {None: (0, size), 0: (0, size // 2), 1: (size // 2, size // 2)}[half]
            return ref.at[yq, pl.ds(pl.multiple_of(c * size + off, 16), n)]

        return piece

    wo_piece, wd_piece = row_piece(wo_all, 128), row_piece(wd_all, 256)
    gu_y = [Gather(net, "y", lambda j: gate_one(j, x, z)), Gather(net, "y", lambda j: up_one(j, x, z))]
    for g in gu_y:
        g.start()
    qkv = Relay(net, "y", qkv_piece, [(qkv_piece(y), qkv_piece(y))])
    w_o = Relay(net, "y", wo_piece, [(wo_piece(y), wo_piece(y))])
    w_d = Relay(net, "y", wd_piece, [(wd_piece(y), wd_piece(y))])
    qkv.start()
    gain_own = gain_all.at[y]
    gain_copies = [net.copy(gain_own, gain_own, "y", s) for s in STEPS]
    for g in gu_y:
        g.end()
    gu_1, gu_2 = [], []
    for s in (1, -1, 2):
        yq = net.at("y", s)
        gu_1.append(Gather(net, "x", lambda j, yq=yq: gate_one(yq, j, z)))
        gu_1.append(Gather(net, "z", lambda j, yq=yq: up_one(yq, x, j)))
        gu_2.append(Gather(net, "z", lambda j, yq=yq: block(yq, j * 512, 512)))
        gu_2.append(Gather(net, "x", lambda j, yq=yq: block(yq, 2048 + j * 512, 512)))
    for g in gu_1:
        g.start()
    for cp in gain_copies:
        cp.wait_recv()
    all_gains = gain_all[...]

    def gain(i, n):
        return jnp.concatenate([all_gains[yq, i : i + 1, :n] for yq in range(4)], axis=1)

    gains[0:1, :] = gain(0, 160)
    for i in range(3, 6):
        gains[i : i + 1, :] = gain(i, 160)
    gains[1:2, 0:256] = gain(1, 64)
    gains[2:3, 0:256] = gain(2, 64)
    g_in, g_q, g_k = gains[0:1, :], gains[1:2, 0:256], gains[2:3, 0:256]
    g_post, g_pre, g_fpost = gains[3:4, :], gains[4:5, :], gains[5:6, :]
    ids = jnp.broadcast_to(positions[...].astype(F32).reshape(1, 128), (128, 128))
    row, col = (lax.broadcasted_iota(jnp.int32, (128, 128), d) for d in (0, 1))
    angles = jnp.sum(jnp.where(row == col, ids, 0.0), axis=1, keepdims=True) * inverse[...]
    cos[...] = jnp.cos(angles)
    sin[...] = jnp.sin(angles)
    t = tokens[...].astype(F32)
    normed_low = (t * rms(t) * g_in).astype(BF)
    normed[own_rows, :] = normed_low

    def share(ref):
        return net.copy(ref.at[own_rows], ref.at[other_rows], "c")

    swaps = {}

    def swap(name, piece, j):
        swaps.setdefault(name, []).append(net.copy(piece(j), piece(j), "c"))

    def swapped(name):
        for cp in swaps[name]:
            cp.wait_recv()

    qkv.mid()
    w_o.start()
    w_d.start()
    swap("qkv", qkv_piece, net.at("y", 1))
    swap("qkv", qkv_piece, net.at("y", -1))
    for a, b in zip(gu_1, gu_2):
        a.end()
    for b in gu_2:
        b.start()
    qkv.end()
    swap("qkv", qkv_piece, net.at("y", 2))
    swapped("qkv")
    both = dot(normed_low, qkv_all[:, :, pl.ds(1024, 512)].reshape(640, 512))
    u = both[:, 0:256]
    raw[:, pl.ds(1024, 256)] = u
    k_all[c, z, x] = rope(u * rms(u) * g_k, cos[...], sin[...]).astype(BF)
    v_all[c, z, x] = both[:, 256:512].astype(BF)
    kx = Gather(net, "x", lambda j: k_all.at[c, z, j])
    vz = Gather(net, "z", lambda j: v_all.at[c, j, x])
    kz = Gather(net, "z", lambda j: k_all.at[c, j])
    vx = Gather(net, "x", lambda j: v_all.at[c, :, j])
    kx.start()
    vz.start()
    both = dot(normed_low, qkv_all[:, :, pl.ds(0, 1024)].reshape(640, 1024))
    raw[:, pl.ds(0, 1024)] = both
    for h in range(4):
        u = both[:, h * 256 : h * 256 + 256]
        q_s[pl.ds(h * 128, 128), :] = (rope(u * rms(u) * g_q, cos[...], sin[...]).astype(BF) * 0.0625).astype(BF)

    def swap_k(j):
        swap("kv", lambda j: k_all.at[c, j], j)

    def swap_v(j):
        swap("kv", lambda j: v_all.at[c, :, j], j)

    kx.end()
    kz.start()
    vz.end()
    vx.start()
    swap_k(z)
    swap_v(x)
    acc[...] = jnp.zeros_like(acc)
    inv_s[...] = jnp.zeros_like(inv_s)
    gain_s[...] = jnp.zeros_like(gain_s)
    ge[:, pl.ds(E_END, E_ROWS - E_END), :] = jnp.zeros((4, E_ROWS - E_END, 128), BF)
    gm[:, pl.ds(M_END, M_ROWS - M_END), :] = jnp.zeros((4, M_ROWS - M_END, 128), BF)
    gl[:, pl.ds(L_END, L_ROWS - L_END), :] = jnp.zeros((4, L_ROWS - L_END, 128), BF)
    shared = {"normed": share(normed)}
    w_o.mid()
    w_d.mid()
    for name, piece in (("wo", wo_piece), ("wd", wd_piece)):
        swap(name, piece, net.at("y", 1))
        swap(name, piece, net.at("y", -1))
    for g in gu_2:
        g.end()
    for s in (1, -1, 2):
        swap("gu", gu_piece, net.at("y", s))
    kz.end(swap_k)
    vx.end(swap_v)
    for r, name, piece in ((w_o, "wo", wo_piece), (w_d, "wd", wd_piece)):
        r.end()
        swap(name, piece, net.at("y", 2))
    swapped("kv")

    def fwd_tile(cc, j, diagonal):
        p = jnp.exp(dot_back(q_s[...], k_all[cc, j].reshape(512, 256)))
        if diagonal:
            p = jnp.where(causal(net, cc), p, 0.0)
        inv_s[...] += jnp.sum(p, axis=1, keepdims=True)
        acc[...] += dot(p.astype(BF), v_all[cc, j].reshape(512, 256))

    def fwd_step(i, _):
        fwd_tile(lax.rem(i, 2), lax.div(i, 2), False)
        return 0

    def fwd_last(i, _):
        fwd_tile(i, z, True)
        return 0

    lax.fori_loop(0, z * 2, fwd_step, 0)
    lax.fori_loop(0, 2, fwd_last, 0)
    inv = 1.0 / inv_s[...]
    inv_s[...] = inv
    acc[...] = acc[...] * inv
    for h in range(4):
        attn[own_rows, pl.ds(h * 256, 256)] = acc[pl.ds(h * 128, 128), :].astype(BF)
    shared["attn"] = share(attn)

    def put_gain(i, value):
        n = value.shape[1] // 4
        for yq in range(4):
            v = value[:, yq * n : yq * n + n]
            gain_s[yq, pl.ds(2 * i, 1), pl.ds(0, min(n, 128))] = v[:, :128]
            if n > 128:
                gain_s[yq, pl.ds(2 * i + 1, 1), pl.ds(0, n - 128)] = v[:, 128:]

    swapped("wo")
    w_out = wo_all[...].reshape(1024, 640)
    proj = dot(attn[own_rows, :], w_out)
    r_proj = rms(proj)
    hidden = tokens[...].astype(F32) + proj * r_proj * g_post
    r_hidden = rms(hidden)
    ffn_low = (hidden * r_hidden * g_pre).astype(BF)
    ffn[own_rows, :] = ffn_low
    shared["ffn"] = share(ffn)
    swapped("gu")
    for i in range(4):
        cs, cs2 = pl.ds(i * 512, 512), pl.ds(2048 + i * 512, 512)
        gate = dot(ffn_low, gu[:, :, cs].reshape(640, 512))
        up = dot(ffn_low, gu[:, :, cs2].reshape(640, 512))
        t = jnp.tanh(C_ROOT * (gate + C_CUBE * gate * gate * gate))
        gelu = 0.5 * gate * (1.0 + t)
        slope = 0.5 * (1.0 + t) + 0.5 * gate * (1.0 - t * t) * (C_ROOT * (1.0 + 3.0 * C_CUBE * gate * gate))
        mixed[own_rows, cs] = (gelu * up).astype(BF)
        f_s[:, cs] = up * slope
        g_s[:, cs] = gelu
    shared["mixed"] = share(mixed)
    swapped("wd")
    down = dot(mixed[own_rows, :], wd_all[...].reshape(2048, 640))
    r_down = rms(down)
    layer_out[...] = (hidden + down * r_down * g_fpost).astype(BF)
    out_grad = cot[...].astype(F32)
    down_grad = norm_back(down, r_down, g_fpost, out_grad).astype(BF)
    put_gain(5, gain_grad(down, r_down, out_grad))
    downg[own_rows, :] = down_grad
    shared["downg"] = share(downg)
    for i in range(4):
        cs, cs2 = pl.ds(i * 512, 512), pl.ds(2048 + i * 512, 512)
        mg = dot_back(down_grad, wd_all[i])
        gug[own_rows, cs] = (mg * f_s[:, cs]).astype(BF)
        gug[own_rows, cs2] = (mg * g_s[:, cs]).astype(BF)
    shared["gug"] = share(gug)
    ffn_grad = dot_back(gug[own_rows, :], gu[...].reshape(640, 4096))
    hidden_grad = out_grad + norm_back(hidden, r_hidden, g_pre, ffn_grad)
    put_gain(4, gain_grad(hidden, r_hidden, ffn_grad))
    hidden_grad_s[...] = hidden_grad
    proj_grad = norm_back(proj, r_proj, g_post, hidden_grad).astype(BF)
    put_gain(3, gain_grad(proj, r_proj, hidden_grad))
    projg[own_rows, :] = proj_grad
    shared["projg"] = share(projg)
    def cols(start, width):
        return pl.ds(pl.multiple_of(start, 128), width)

    def put(g, off, n, value, col_blocks):
        value = value.astype(BF)
        for yq in range(4):
            for j in range(col_blocks):
                g[yq, pl.ds(off + j * n, n), :] = value[yq * n : yq * n + n, j * 128 : j * 128 + 128]

    for name in ("ffn", "gug"):
        shared[name].wait_recv()
    for part in range(2):
        put(ge, OFF_G + part * 640, 160, tdot(ffn[...], gug[:, cols(c * 1024 + part * 512, 512)]), 4)
        put(ge, OFF_U + part * 640, 160, tdot(ffn[...], gug[:, cols(2048 + c * 1024 + part * 512, 512)]), 4)
    early_a = Group(net, ge, e_full, EA_PARTS, group_b[0], relay=True)
    early_a.step()
    attn_grad = dot_back(proj_grad, w_out).astype(BF)
    for h in range(4):
        do_s[pl.ds(h * 128, 128), :] = attn_grad[:, h * 256 : h * 256 + 256]
    delta_s[...] = jnp.sum(do_s[...].astype(F32) * acc[...], axis=1, keepdims=True)

    for name in ("attn", "mixed", "downg", "projg"):
        shared[name].wait_recv()
    for yq in range(4):
        value = tdot(attn[:, cols(yq * 256 + c * 128, 128)], projg[...]).astype(BF)
        for j in range(5):
            ge[yq, pl.ds(OFF_O + j * 128, 128), :] = value[:, j * 128 : j * 128 + 128]
        value = tdot(mixed[:, cols(yq * 512 + c * 256, 256)], downg[...]).astype(BF)
        for j in range(5):
            ge[yq, pl.ds(OFF_D + j * 256, 256), :] = value[:, j * 128 : j * 128 + 128]
    early_b = Group(net, ge, e_full, EB_PARTS, group_b[1])
    early_b.step()

    acc[...] = jnp.zeros_like(acc)

    def tile(cc, j, diagonal):
        kt, vt = k_all[cc, j].reshape(512, 256), v_all[cc, j].reshape(512, 256)
        p = jnp.exp(dot_back(q_s[...], kt)) * inv_s[...]
        if diagonal:
            p = jnp.where(causal(net, cc), p, 0.0)
        ds = (p * (dot_back(do_s[...], vt) - delta_s[...])).astype(BF)
        acc[...] += dot(ds, kt)
        dk[cc, j] = tdot(ds, q_s[...]).astype(BF).reshape(4, 128, 256)
        dv[cc, j] = tdot(p.astype(BF), do_s[...]).astype(BF).reshape(4, 128, 256)

    kc, vc = {}, {}

    def tiles(s):
        j = net.at("z", s)

        def step(i, _):
            cc = lax.rem(other + i, 2)
            if s == 0:
                tile(cc, j, True)
            else:

                @pl.when(j < z)
                def _():
                    tile(cc, j, False)

                @pl.when(j > z)
                def _():
                    dk[cc, j] = jnp.zeros((4, 128, 256), BF)
                    dv[cc, j] = jnp.zeros((4, 128, 256), BF)

            return 0

        lax.fori_loop(0, 2, step, 0)
        kc[s] = net.copy(dk.at[other, j], kin.at[j], "c")
        vc[s] = net.copy(dv.at[other, j], vin.at[j], "c")

    k1 = Scatter(net, "z", lambda j: kin.at[j], kbufs)
    v1 = Scatter(net, "x", lambda j: vin.at[:, j], vbufs)
    k2 = Scatter(net, "x", lambda j: kin.at[z, j], k2bufs)
    v2 = Scatter(net, "z", lambda j: vin.at[j, x], v2bufs)

    def take(s):
        j = net.at("z", s)
        kc[s].wait_recv()
        add_rows(kin.at[j], (dk.at[c, j],))
        if s != 0:
            k1.send(s)
        vc[s].wait_recv()
        add_rows(vin.at[j], (dv.at[c, j],))

    tiles(2)
    tiles(1)
    take(2)
    tiles(-1)
    take(1)
    early_a.mid()
    tiles(0)
    take(-1)
    take(0)
    v1.start()

    total_q = jnp.zeros((1, 256), F32)
    for h in range(4):
        v = raw[:, pl.ds(h * 256, 256)]
        r = rms(v)
        u = rope_back(acc[pl.ds(h * 128, 128), :] * 0.0625, cos[...], sin[...])
        total_q += gain_grad(v, r, u)
        qkvg[own_rows, pl.ds(h * 256, 256)] = norm_back(v, r, g_q, u).astype(BF)
    put_gain(1, total_q)
    q_cols, kv_cols = pl.ds(0, 1024), pl.ds(1024, 512)
    share_q = net.copy(qkvg.at[own_rows, q_cols], qkvg.at[other_rows, q_cols], "c")
    normed_grad = dot_back(qkvg[own_rows, q_cols], qkv_all[:, :, q_cols].reshape(640, 1024))
    early_b.step()
    shared["normed"].wait_recv()
    share_q.wait_recv()
    put(gm, OFF_Q, 160, tdot(normed[...], qkvg[:, cols(c * 512, 512)]), 4)
    middle = Group(net, gm, m_full, M_PARTS, group_b[2])
    k1.end()
    k2.start()
    v1.end()
    v2.start()
    middle.step()
    early_b.step()
    k2.end()
    v2.end()
    early_a.step()

    v = raw[:, pl.ds(1024, 256)]
    r = rms(v)
    u = rope_back(kin[z, x].astype(F32), cos[...], sin[...])
    put_gain(2, gain_grad(v, r, u))
    qkvg[own_rows, pl.ds(1024, 256)] = norm_back(v, r, g_k, u).astype(BF)
    qkvg[own_rows, pl.ds(1280, 256)] = vin[z, x]
    share_kv = net.copy(qkvg.at[own_rows, kv_cols], qkvg.at[other_rows, kv_cols], "c")
    normed_grad = normed_grad + dot_back(qkvg[own_rows, kv_cols], qkv_all[:, :, kv_cols].reshape(640, 512))
    t = tokens[...].astype(F32)
    r = rms(t)
    put_gain(0, gain_grad(t, r, normed_grad))
    gain_copy = net.copy(gain_s, gain_other, "c")
    input_grad[...] = hidden_grad_s[...] + norm_back(t, r, g_in, normed_grad)
    middle.step()
    share_kv.wait_recv()
    put(gl, OFF_K, 160, tdot(normed[...], qkvg[:, cols(1024 + c * 128, 128)]), 1)
    put(gl, OFF_V, 160, tdot(normed[...], qkvg[:, cols(1280 + c * 128, 128)]), 1)
    gain_copy.wait_recv()
    gl[:, pl.ds(OFF_GAIN, 16), :] = (gain_s[...] + gain_other[...]).astype(BF)
    late = Group(net, gl, l_full, L_PARTS, group_b[3])
    late.step()
    early_a.step()
    early_b.step()
    middle.step()
    late.step()
    early_a.step()
    early_b.step()
    middle.step()
    late.step()
    early_a.step()
    early_b.step()
    middle.step()
    late.step()
    early_a.step()
    middle.step()
    late.step()
    early_a.step()
    late.step()
    early_b.step()
    e_copy = pltpu.make_async_copy(e_full, e_out, own_sem.at[0])
    e_copy.start()
    middle.step()
    m_copy = pltpu.make_async_copy(m_full, m_out, own_sem.at[1])
    m_copy.start()
    late.step()
    e_copy.wait()
    m_copy.wait()
    net.drain()


def layer(*args):
    def s(dtype, *shape):
        return jax.ShapeDtypeStruct(shape, dtype)

    n = 6 + 4 + 3 + 18 + 18 + 3 + 4 + 4 + 3 + 3 + 3 + 12 + 8 + 8 + 2 + 8 + 12 + sum(16 * len(p) + 1 for p in ALL_PARTS)
    big, small = VMEM((4, 128, 256), BF), VMEM((128, 256), BF)
    whole = VMEM((2, 4, 4, 128, 256), BF)
    column = VMEM((512, 1), F32)
    return pl.pallas_call(
        layer_kernel,
        out_shape=(
            s(BF, 128, 640), s(F32, 128, 640), s(BF, 2, E_ROWS, 128), s(BF, 2, M_ROWS, 128), s(BF, 2, L_ROWS, 128)
        ),
        in_specs=[ANYSPEC] * 7 + [VSPEC] * 10,
        out_specs=[VSPEC, VSPEC, ANYSPEC, ANYSPEC, VSPEC],
        scratch_shapes=[
            VMEM((2, E_ROWS, 128), BF), VMEM((2, M_ROWS, 128), BF),
            VMEM((4, 160, 1536), BF), VMEM((4, 160, 4096), BF), VMEM((4, 256, 640), BF), VMEM((4, 512, 640), BF),
            whole, whole,
            *[VMEM((256, n), BF) for n in (640, 1536, 1024, 640, 640, 4096, 2048, 640)],
            VMEM((4, 8, 256), F32), VMEM((8, 640), F32), VMEM((4, 16, 128), F32), VMEM((4, 16, 128), F32),
            VMEM((4, E_ROWS, 128), BF), VMEM((4, M_ROWS, 128), BF), VMEM((4, L_ROWS, 128), BF),
            VMEM((128, 128), F32), VMEM((128, 128), F32),
            whole, whole, VMEM((4, 4, 128, 256), BF), VMEM((4, 4, 128, 256), BF),
            VMEM((512, 256), F32), column, column, VMEM((512, 256), BF), VMEM((512, 256), BF), VMEM((128, 1280), F32),
            VMEM((128, 2048), F32), VMEM((128, 2048), F32), VMEM((128, 640), F32),
            *[big] * 6, *[small] * 6,
            *[b for parts in ALL_PARTS for b in group_bufs(parts)],
            pltpu.SemaphoreType.DMA((n,)),
            pltpu.SemaphoreType.DMA((n,)),
            pltpu.SemaphoreType.DMA((7,)),
        ],
        compiler_params=pltpu.CompilerParams(collective_id=0, has_side_effects=True, vmem_limit_bytes=VMEM_LIMIT),
        name="layer",
    )(*args)


def unpack_kernel(e, m, l, lo, ig, lo_out, ig_out, oq, ok, ov, oo, og, ou, od, *gain_outs):
    lo_out[...] = lo[...]
    ig_out[...] = ig[...]
    for c in range(2):

        def block(full, off, n, j):
            return full[c, pl.ds(off + j * n, n), :].astype(F32)

        for j in range(4):
            oq[:, pl.ds(c * 512 + j * 128, 128)] = block(m, OFF_Q, 160, j)
        ok[:, pl.ds(c * 128, 128)] = block(l, OFF_K, 160, 0)
        ov[:, pl.ds(c * 128, 128)] = block(l, OFF_V, 160, 0)
        for j in range(8):
            og[:, pl.ds(c * 1024 + j * 128, 128)] = block(e, OFF_G, 160, j)
            ou[:, pl.ds(c * 1024 + j * 128, 128)] = block(e, OFF_U, 160, j)
        for j in range(5):
            oo[pl.ds(c * 128, 128), pl.ds(j * 128, 128)] = block(e, OFF_O, 128, j)
            od[pl.ds(c * 256, 256), pl.ds(j * 128, 128)] = block(e, OFF_D, 256, j)
    rows = l[0, pl.ds(OFF_GAIN, 16), :].astype(F32)
    for i, n in enumerate(GAIN_SIZES):
        gain_outs[i][:, pl.ds(0, min(n, 128))] = rows[2 * i : 2 * i + 1, : min(n, 128)]
        if n > 128:
            gain_outs[i][:, pl.ds(128, n - 128)] = rows[2 * i + 1 : 2 * i + 2, : n - 128]


def unpack(e, m, l, lo, ig):
    def s(*shape):
        return jax.ShapeDtypeStruct(shape, F32)

    return pl.pallas_call(
        unpack_kernel,
        out_shape=(
            jax.ShapeDtypeStruct((128, 640), BF), s(128, 640), s(160, 1024), s(160, 256), s(160, 256), s(256, 640), s(160, 2048), s(160, 2048), s(512, 640),
            *[s(1, n) for n in GAIN_SIZES],
        ),
        in_specs=[VSPEC] * 5,
        out_specs=[VSPEC] * 15,
        compiler_params=pltpu.CompilerParams(vmem_limit_bytes=VMEM_LIMIT),
        name="unpack",
    )(e, m, l, lo, ig)


def local(
    tokens, positions, w_query, w_key, w_value, w_out, w_gate, w_up, w_down,
    gain_in, gain_query, gain_key, gain_attn_post, gain_ffn_pre, gain_ffn_post, cotangent,
):
    gains = (gain_in, gain_query, gain_key, gain_attn_post, gain_ffn_pre, gain_ffn_post)
    exponents = jnp.arange(0, 256, 2, dtype=F32) / 256
    inverse = 1.0 / ROPE_BASE**exponents
    layer_out, input_grad, e_full, m_full, l_full = layer(
        w_query, w_key, w_value, w_out, w_gate, w_up, w_down, *gains, tokens, cotangent, positions, inverse.reshape(1, 128)
    )
    layer_out, input_grad, oq, ok, ov, oo, og, ou, od, *gain_grads = unpack(e_full, m_full, l_full, layer_out, input_grad)
    return (layer_out, input_grad, oq, ok, ov, oo, og, ou, od, *[g.reshape(g.shape[1]) for g in gain_grads])


def solution(mesh):
    rows, both, vec = P("fsdp", None), P(("fsdp", "ctx"), None), P("fsdp")
    in_specs = (both, P(("fsdp", "ctx")), *[rows] * 7, *[vec] * 6, both)
    out_specs = (both, both, *[rows] * 7, *[vec] * 6)
    return jax.shard_map(local, mesh=mesh, in_specs=in_specs, out_specs=out_specs, check_vma=False)
```

```python
import functools

import jax
import jax.numpy as jnp
from jax import lax
from jax.experimental import pallas as pl
from jax.experimental.pallas import tpu as pltpu
from jax.sharding import PartitionSpec as P

EPS = 1e-06
ROPE_BASE = 1000000.0
BF = jnp.bfloat16
F32 = jnp.float32
MESH = pl.DeviceIdType.MESH
VMEM = pltpu.VMEM
VSPEC = pl.BlockSpec(memory_space=pltpu.VMEM)
ANYSPEC = pl.BlockSpec(memory_space=pl.ANY)
VMEM_LIMIT = 60 * 1024 * 1024
C_ROOT = 0.7978845608028654
C_CUBE = 0.044715

E_ROWS, M_ROWS, L_ROWS = 4608, 768, 512
OFF_G, OFF_U, OFF_O, OFF_D, E_END = 0, 1280, 2560, 3200, 4480
OFF_Q, M_END = 0, 640
OFF_K, OFF_V, OFF_GAIN, L_END = 0, 160, 320, 336
EA_PARTS = ((0, 1280, "yzx"), (1280, 1280, "yxz"))
EB_PARTS = ((2560, 1024, "xzy"), (3584, 1024, "zxy"))
M_PARTS = ((0, 256, "yzx"), (256, 256, "xzy"), (512, 256, "zxy"))
L_PARTS = ((0, 256, "yzx"), (256, 256, "xyz"))
GAIN_SIZES = (160, 64, 64, 160, 160, 160)
STEPS = (2, 1, -1)


class Net:
    def __init__(self, send_sem, recv_sem):
        me = lax.axis_index("ctx")
        self.y = lax.axis_index("fsdp")
        self.c = lax.rem(me, 2)
        self.x = lax.rem(lax.div(me, 2), 4)
        self.z = lax.div(me, 8)
        self.send_sem, self.recv_sem = send_sem, recv_sem
        self.used = 0
        self.sent = []

    def pos(self, axis):
        return {"x": self.x, "y": self.y, "z": self.z}[axis]

    def at(self, axis, step):
        return lax.rem(self.pos(axis) + (step + 4), 4)

    def dev(self, axis, step):
        x, y, z, c = self.x, self.y, self.z, self.c
        if axis == "x":
            x = self.at("x", step)
        elif axis == "y":
            y = self.at("y", step)
        elif axis == "z":
            z = self.at("z", step)
        else:
            c = 1 - c
        return {"fsdp": y, "ctx": z * 8 + x * 2 + c}

    def copy(self, src, dst, axis, step=1):
        k = self.used
        self.used += 1
        cp = pltpu.make_async_remote_copy(
            src_ref=src,
            dst_ref=dst,
            send_sem=self.send_sem.at[k],
            recv_sem=self.recv_sem.at[k],
            device_id=self.dev(axis, step),
            device_id_type=MESH,
        )
        cp.start()
        self.sent.append(cp)
        return cp

    def barrier(self):
        sem = pltpu.get_barrier_semaphore()
        peers = [("c", 1), *[(a, s) for a in "xyz" for s in STEPS]]
        for axis, step in peers:
            pl.semaphore_signal(sem, inc=1, device_id=self.dev(axis, step), device_id_type=MESH)
        pl.semaphore_wait(sem, len(peers))

    def drain(self):
        for cp in self.sent:
            cp.wait_send()


class Relay:
    def __init__(self, net, axis, piece, own):
        self.net, self.axis, self.piece, self.own = net, axis, piece, own

    def start(self):
        self.up = [self.net.copy(a, b, self.axis, 1) for a, b in self.own]
        self.down = [self.net.copy(a, b, self.axis, -1) for a, b in self.own]

    def mid(self):
        for cp in self.up:
            cp.wait_recv()
        low = self.piece(self.net.at(self.axis, -1), 0)
        self.up2 = self.net.copy(low, low, self.axis, 1)
        for cp in self.down:
            cp.wait_recv()
        high = self.piece(self.net.at(self.axis, 1), 1)
        self.down2 = self.net.copy(high, high, self.axis, -1)

    def end(self):
        self.up2.wait_recv()
        self.down2.wait_recv()


class Gather:
    def __init__(self, net, axis, piece):
        self.net, self.axis, self.piece = net, axis, piece

    def start(self):
        own = self.piece(self.net.pos(self.axis))
        self.copies = [(s, self.net.copy(own, own, self.axis, s)) for s in (1, -1, 2)]

    def end(self, then=None):
        for s, cp in self.copies:
            cp.wait_recv()
            if then is not None:
                then(self.net.at(self.axis, -s))


class RelayScatter:
    def __init__(self, net, axis, q, bufs):
        self.net, self.axis, self.q, self.bufs = net, axis, q, bufs
        self.n = bufs[0].shape[1] // 2

    def half(self, ref, h):
        return ref.at[:, pl.ds(h * self.n, self.n)]

    def start(self):
        far = self.q(self.net.at(self.axis, 2))
        first = self.bufs[0]
        self.cl = self.net.copy(self.half(far, 0), self.half(first, 0), self.axis, 1)
        self.ch = self.net.copy(self.half(far, 1), self.half(first, 1), self.axis, -1)

    def mid(self):
        up, down = self.q(self.net.at(self.axis, 1)), self.q(self.net.at(self.axis, -1))
        first = self.bufs[0]
        self.cl.wait_recv()
        add_rows(self.half(up, 0), (self.half(first, 0),))
        self.cp = self.net.copy(up, self.bufs[1], self.axis, 1)
        self.ch.wait_recv()
        add_rows(self.half(down, 1), (self.half(first, 1),))
        self.cm = self.net.copy(down, self.bufs[2], self.axis, -1)

    def end(self, out=None):
        self.cp.wait_recv()
        self.cm.wait_recv()
        add_rows(self.q(self.net.pos(self.axis)), self.bufs[1:], out)


class Scatter:
    def __init__(self, net, axis, q, bufs):
        self.net, self.axis, self.q, self.bufs = net, axis, q, bufs
        self.copies = []

    def send(self, s):
        buf = self.bufs[STEPS.index(s)]
        self.copies.append(self.net.copy(self.q(self.net.at(self.axis, s)), buf, self.axis, s))

    def start(self):
        for s in STEPS:
            self.send(s)

    def end(self, out=None):
        for cp in self.copies:
            cp.wait_recv()
        add_rows(self.q(self.net.pos(self.axis)), self.bufs, out)


def add_rows(dst, srcs, out=None):
    target = dst if out is None else out
    lead, rows = dst.shape[:-2], dst.shape[-2]
    step = next(n for n in (256, 192, 128, 96, 64, 48, 32, 16) if rows % n == 0)
    per = rows // step
    count = per
    for n in lead:
        count *= n

    def body(i, _):
        idx = []
        k = lax.div(i, per)
        for n in reversed(lead):
            idx.insert(0, lax.rem(k, n))
            k = lax.div(k, n)
        idx = (*idx, pl.ds(pl.multiple_of(lax.rem(i, per) * step, 16), step), slice(None))
        total = dst[idx].astype(F32)
        for s in srcs:
            total += s[idx].astype(F32)
        target[idx] = total.astype(target.dtype)
        return 0

    lax.fori_loop(0, count, body, 0)


def tdot(a, b):
    return lax.dot_general(a, b, (((0,), (0,)), ((), ())), preferred_element_type=F32)


def dot(a, b):
    return jnp.dot(a, b, preferred_element_type=F32)


def dot_back(a, b):
    return lax.dot_general(a, b, (((1,), (1,)), ((), ())), preferred_element_type=F32)


def rms(v):
    return lax.rsqrt(jnp.mean(v * v, axis=-1, keepdims=True) + EPS)


def norm_back(v, r, g, u):
    ug = u * g
    return r * ug - v * (r * r * r) * jnp.mean(ug * v, axis=-1, keepdims=True)


def gain_grad(v, r, u):
    return jnp.sum(u * v * r, axis=0, keepdims=True)


def rope(u, cos, sin):
    a, b = u[:, :128], u[:, 128:]
    return jnp.concatenate([a * cos - b * sin, b * cos + a * sin], axis=1)


def rope_back(w, cos, sin):
    a, b = w[:, :128], w[:, 128:]
    return jnp.concatenate([a * cos + b * sin, b * cos - a * sin], axis=1)


def causal(net, c_key):
    row = lax.broadcasted_iota(jnp.int32, (512, 512), 0)
    col = lax.broadcasted_iota(jnp.int32, (512, 512), 1)
    q_pos = (net.x * 2 + net.c) * 128 + (row & 127)
    k_pos = (col >> 7) * 256 + c_key * 128 + (col & 127)
    return k_pos <= q_pos


class Group:
    def __init__(self, net, g, full, parts, bufs, relay=False):
        self.relay = relay
        self.net, self.g, self.full, self.parts, self.bufs = net, g, full, parts, bufs
        self.place = [[0, 4, off, rows] for off, rows, _ in parts]
        self.phase = -1

    def q(self, p, axis):
        y0, yn, r0, rn = self.place[p]

        def share(j):
            if axis == "y":
                return self.g.at[pl.ds(j, 1), pl.ds(pl.multiple_of(r0, 16), rn)]
            return self.g.at[pl.ds(y0, yn), pl.ds(pl.multiple_of(r0 + j * (rn // 4), 16), rn // 4)]

        return share

    def scatter_start(self, phase):
        self.runs = []
        for p, (_, _, order) in enumerate(self.parts):
            k = (p * 3 + phase) * 3
            kind = RelayScatter if self.relay and phase == 0 else Scatter
            self.runs.append(kind(self.net, order[phase], self.q(p, order[phase]), self.bufs[k : k + 3]))
            self.runs[-1].start()

    def scatter_end(self, phase):
        for p, r in enumerate(self.runs):
            y0, yn, r0, rn = self.place[p]
            axis = self.parts[p][2][phase]
            if axis == "y":
                self.place[p] = [self.net.y, 1, r0, rn]
            else:
                self.place[p] = [y0, yn, r0 + self.net.pos(axis) * (rn // 4), rn // 4]
            _, _, r0, rn = self.place[p]
            r.end(self.full.at[pl.ds(self.net.c, 1), pl.ds(pl.multiple_of(r0, 16), rn)] if phase == 2 else None)

    def mid(self):
        for r in self.runs:
            r.mid()

    def gather_start(self, stage):
        self.runs = []
        for off, rows, order in self.parts:
            u = rows // 16
            major, minor = order.replace("y", "")

            def piece(j, u=u, off=off, major=major):
                if stage == 0:
                    return self.full.at[self.net.c, pl.ds(pl.multiple_of(off + self.net.pos(major) * 4 * u + j * u, 16), u)]
                return self.full.at[self.net.c, pl.ds(pl.multiple_of(off + j * 4 * u, 16), 4 * u)]

            self.runs.append(Gather(self.net, minor if stage == 0 else major, piece))
            self.runs[-1].start()

    def step(self):
        done, self.phase = self.phase, self.phase + 1
        if 0 <= done < 3:
            self.scatter_end(done)
        elif 3 <= done < 5:
            for r in self.runs:
                r.end()
        elif done == 5:
            self.swap.wait_recv()
        if done < 2:
            self.scatter_start(done + 1)
        elif done < 4:
            self.gather_start(done - 2)
        elif done == 4:
            ref = self.full.at[self.net.c, pl.ds(self.parts[0][0], sum(rows for _, rows, _ in self.parts))]
            self.swap = self.net.copy(ref, ref, "c")


def group_bufs(parts):
    bufs = []
    for _, rows, order in parts:
        lead = 4
        for axis in order:
            if axis == "y":
                lead = 1
            else:
                rows //= 4
            bufs += [VMEM((lead, rows, 128), BF)] * 3
    return bufs


ALL_PARTS = (EA_PARTS, EB_PARTS, M_PARTS, L_PARTS)


def layer_kernel(*refs):
    refs = list(refs)

    def take_refs(n):
        out = refs[:n]
        del refs[:n]
        return out

    wq, wk, wv, wo, wg, wu, wd = take_refs(7)
    gain_ins = take_refs(6)
    tokens_in, cot_in, positions, inverse = take_refs(4)
    layer_out, input_grad, e_out, m_out, l_full = take_refs(5)
    e_full, m_full = take_refs(2)
    qkv_all, gu, wo_all, wd_all, k_all, v_all = take_refs(6)
    normed, qkvg, attn, projg, ffn, gug, mixed, downg = take_refs(8)
    gain_all, gains, gain_s, gain_other, ge, gm, gl = take_refs(7)
    cos, sin, tokens, cot = take_refs(4)
    dk, dv, kin, vin, acc, inv_s, delta_s, do_s, q_s, raw, f_s, g_s, hidden_grad_s = take_refs(13)
    kbufs, vbufs, k2bufs, v2bufs = take_refs(3), take_refs(3), take_refs(3), take_refs(3)
    group_b = [take_refs(9 * len(parts)) for parts in ALL_PARTS]
    send_sem, recv_sem, own_sem = take_refs(3)
    net = Net(send_sem, recv_sem)
    y, c, x, z = net.y, net.c, net.x, net.z
    other = 1 - c
    own_rows, other_rows = pl.ds(0, 128), pl.ds(128, 128)
    own = []
    for k, (src, dst) in enumerate(
        [
            (wg, gu.at[y, :, pl.ds(0, 2048)]), (wu, gu.at[y, :, pl.ds(2048, 2048)]),
            (wq, qkv_all.at[y, :, pl.ds(0, 1024)]), (wk, qkv_all.at[y, :, pl.ds(1024, 256)]),
            (wv, qkv_all.at[y, :, pl.ds(1280, 256)]), (wo, wo_all.at[y]), (wd, wd_all.at[y]),
            (tokens_in, tokens), (cot_in, cot),
        ]
    ):
        own.append(pltpu.make_async_copy(src, dst, own_sem.at[k]))
        own[-1].start()
    gain_all[y] = jnp.zeros((8, 256), F32)
    for i, n in enumerate(GAIN_SIZES):
        gain_all[y, pl.ds(i, 1), pl.ds(0, n)] = gain_ins[i][...].astype(F32).reshape(1, n)
    net.barrier()
    for cp in own:
        cp.wait()

    rows = pl.ds(pl.multiple_of(c * 80, 16), 80)

    def block(yq, start, n):
        return gu.at[yq, rows, pl.ds(pl.multiple_of(start, 128), n)]

    def gate_one(yq, xj, zj):
        return block(yq, (zj * 4 + xj) * 128, 128)

    def up_one(yq, xj, zj):
        return block(yq, 2048 + (xj * 4 + zj) * 128, 128)

    def qkv_piece(yq, half=None):
        off, n = {None: (0, 1536), 0: (0, 768), 1: (768, 768)}[half]
        return qkv_all.at[yq, rows, pl.ds(off, n)]

    def gu_piece(yq):
        return gu.at[yq, rows]

    def row_piece(ref, size):
        def piece(yq, half=None):
            off, n = {None: (0, size), 0: (0, size // 2), 1: (size // 2, size // 2)}[half]
            return ref.at[yq, pl.ds(pl.multiple_of(c * size + off, 16), n)]

        return piece

    wo_piece, wd_piece = row_piece(wo_all, 128), row_piece(wd_all, 256)
    gu_y = [Gather(net, "y", lambda j: gate_one(j, x, z)), Gather(net, "y", lambda j: up_one(j, x, z))]
    for g in gu_y:
        g.start()
    qkv = Relay(net, "y", qkv_piece, [(qkv_piece(y), qkv_piece(y))])
    w_o = Relay(net, "y", wo_piece, [(wo_piece(y), wo_piece(y))])
    w_d = Relay(net, "y", wd_piece, [(wd_piece(y), wd_piece(y))])
    qkv.start()
    gain_own = gain_all.at[y]
    gain_copies = [net.copy(gain_own, gain_own, "y", s) for s in STEPS]
    for g in gu_y:
        g.end()
    gu_1, gu_2 = [], []
    for s in (1, -1, 2):
        yq = net.at("y", s)
        gu_1.append(Gather(net, "x", lambda j, yq=yq: gate_one(yq, j, z)))
        gu_1.append(Gather(net, "z", lambda j, yq=yq: up_one(yq, x, j)))
        gu_2.append(Gather(net, "z", lambda j, yq=yq: block(yq, j * 512, 512)))
        gu_2.append(Gather(net, "x", lambda j, yq=yq: block(yq, 2048 + j * 512, 512)))
    for g in gu_1:
        g.start()
    for cp in gain_copies:
        cp.wait_recv()
    all_gains = gain_all[...]

    def gain(i, n):
        return jnp.concatenate([all_gains[yq, i : i + 1, :n] for yq in range(4)], axis=1)

    gains[0:1, :] = gain(0, 160)
    for i in range(3, 6):
        gains[i : i + 1, :] = gain(i, 160)
    gains[1:2, 0:256] = gain(1, 64)
    gains[2:3, 0:256] = gain(2, 64)
    g_in, g_q, g_k = gains[0:1, :], gains[1:2, 0:256], gains[2:3, 0:256]
    g_post, g_pre, g_fpost = gains[3:4, :], gains[4:5, :], gains[5:6, :]
    ids = jnp.broadcast_to(positions[...].astype(F32).reshape(1, 128), (128, 128))
    row, col = (lax.broadcasted_iota(jnp.int32, (128, 128), d) for d in (0, 1))
    angles = jnp.sum(jnp.where(row == col, ids, 0.0), axis=1, keepdims=True) * inverse[...]
    cos[...] = jnp.cos(angles)
    sin[...] = jnp.sin(angles)
    t = tokens[...].astype(F32)
    normed_low = (t * rms(t) * g_in).astype(BF)
    normed[own_rows, :] = normed_low

    def share(ref):
        return net.copy(ref.at[own_rows], ref.at[other_rows], "c")

    swaps = {}

    def swap(name, piece, j):
        swaps.setdefault(name, []).append(net.copy(piece(j), piece(j), "c"))

    def swapped(name):
        for cp in swaps[name]:
            cp.wait_recv()

    qkv.mid()
    w_o.start()
    w_d.start()
    swap("qkv", qkv_piece, net.at("y", 1))
    swap("qkv", qkv_piece, net.at("y", -1))
    for a, b in zip(gu_1, gu_2):
        a.end()
    for b in gu_2:
        b.start()
    qkv.end()
    swap("qkv", qkv_piece, net.at("y", 2))
    swapped("qkv")
    both = dot(normed_low, qkv_all[:, :, pl.ds(1024, 512)].reshape(640, 512))
    u = both[:, 0:256]
    raw[:, pl.ds(1024, 256)] = u
    k_all[c, z, x] = rope(u * rms(u) * g_k, cos[...], sin[...]).astype(BF)
    v_all[c, z, x] = both[:, 256:512].astype(BF)
    kx = Gather(net, "x", lambda j: k_all.at[c, z, j])
    vz = Gather(net, "z", lambda j: v_all.at[c, j, x])
    kz = Gather(net, "z", lambda j: k_all.at[c, j])
    vx = Gather(net, "x", lambda j: v_all.at[c, :, j])
    kx.start()
    vz.start()
    both = dot(normed_low, qkv_all[:, :, pl.ds(0, 1024)].reshape(640, 1024))
    raw[:, pl.ds(0, 1024)] = both
    for h in range(4):
        u = both[:, h * 256 : h * 256 + 256]
        q_s[pl.ds(h * 128, 128), :] = (rope(u * rms(u) * g_q, cos[...], sin[...]).astype(BF) * 0.0625).astype(BF)

    def swap_k(j):
        swap("kv", lambda j: k_all.at[c, j], j)

    def swap_v(j):
        swap("kv", lambda j: v_all.at[c, :, j], j)

    kx.end()
    kz.start()
    vz.end()
    vx.start()
    swap_k(z)
    swap_v(x)
    acc[...] = jnp.zeros_like(acc)
    inv_s[...] = jnp.zeros_like(inv_s)
    gain_s[...] = jnp.zeros_like(gain_s)
    ge[:, pl.ds(E_END, E_ROWS - E_END), :] = jnp.zeros((4, E_ROWS - E_END, 128), BF)
    gm[:, pl.ds(M_END, M_ROWS - M_END), :] = jnp.zeros((4, M_ROWS - M_END, 128), BF)
    gl[:, pl.ds(L_END, L_ROWS - L_END), :] = jnp.zeros((4, L_ROWS - L_END, 128), BF)
    shared = {"normed": share(normed)}
    w_o.mid()
    w_d.mid()
    for name, piece in (("wo", wo_piece), ("wd", wd_piece)):
        swap(name, piece, net.at("y", 1))
        swap(name, piece, net.at("y", -1))
    for g in gu_2:
        g.end()
    for s in (1, -1, 2):
        swap("gu", gu_piece, net.at("y", s))
    kz.end(swap_k)
    vx.end(swap_v)
    for r, name, piece in ((w_o, "wo", wo_piece), (w_d, "wd", wd_piece)):
        r.end()
        swap(name, piece, net.at("y", 2))
    swapped("kv")

    def fwd_tile(cc, j, diagonal):
        p = jnp.exp(dot_back(q_s[...], k_all[cc, j].reshape(512, 256)))
        if diagonal:
            p = jnp.where(causal(net, cc), p, 0.0)
        inv_s[...] += jnp.sum(p, axis=1, keepdims=True)
        acc[...] += dot(p.astype(BF), v_all[cc, j].reshape(512, 256))

    def fwd_step(i, _):
        fwd_tile(lax.rem(i, 2), lax.div(i, 2), False)
        return 0

    def fwd_last(i, _):
        fwd_tile(i, z, True)
        return 0

    lax.fori_loop(0, z * 2, fwd_step, 0)
    lax.fori_loop(0, 2, fwd_last, 0)
    inv = 1.0 / inv_s[...]
    inv_s[...] = inv
    acc[...] = acc[...] * inv
    for h in range(4):
        attn[own_rows, pl.ds(h * 256, 256)] = acc[pl.ds(h * 128, 128), :].astype(BF)
    shared["attn"] = share(attn)

    def put_gain(i, value):
        n = value.shape[1] // 4
        for yq in range(4):
            v = value[:, yq * n : yq * n + n]
            gain_s[yq, pl.ds(2 * i, 1), pl.ds(0, min(n, 128))] = v[:, :128]
            if n > 128:
                gain_s[yq, pl.ds(2 * i + 1, 1), pl.ds(0, n - 128)] = v[:, 128:]

    swapped("wo")
    w_out = wo_all[...].reshape(1024, 640)
    proj = dot(attn[own_rows, :], w_out)
    r_proj = rms(proj)
    hidden = tokens[...].astype(F32) + proj * r_proj * g_post
    r_hidden = rms(hidden)
    ffn_low = (hidden * r_hidden * g_pre).astype(BF)
    ffn[own_rows, :] = ffn_low
    shared["ffn"] = share(ffn)
    swapped("gu")
    for i in range(4):
        cs, cs2 = pl.ds(i * 512, 512), pl.ds(2048 + i * 512, 512)
        gate = dot(ffn_low, gu[:, :, cs].reshape(640, 512))
        up = dot(ffn_low, gu[:, :, cs2].reshape(640, 512))
        t = jnp.tanh(C_ROOT * (gate + C_CUBE * gate * gate * gate))
        gelu = 0.5 * gate * (1.0 + t)
        slope = 0.5 * (1.0 + t) + 0.5 * gate * (1.0 - t * t) * (C_ROOT * (1.0 + 3.0 * C_CUBE * gate * gate))
        mixed[own_rows, cs] = (gelu * up).astype(BF)
        f_s[:, cs] = up * slope
        g_s[:, cs] = gelu
    shared["mixed"] = share(mixed)
    swapped("wd")
    down = dot(mixed[own_rows, :], wd_all[...].reshape(2048, 640))
    r_down = rms(down)
    layer_out[...] = (hidden + down * r_down * g_fpost).astype(BF)
    out_grad = cot[...].astype(F32)
    down_grad = norm_back(down, r_down, g_fpost, out_grad).astype(BF)
    put_gain(5, gain_grad(down, r_down, out_grad))
    downg[own_rows, :] = down_grad
    shared["downg"] = share(downg)
    for i in range(4):
        cs, cs2 = pl.ds(i * 512, 512), pl.ds(2048 + i * 512, 512)
        mg = dot_back(down_grad, wd_all[i])
        gug[own_rows, cs] = (mg * f_s[:, cs]).astype(BF)
        gug[own_rows, cs2] = (mg * g_s[:, cs]).astype(BF)
    shared["gug"] = share(gug)
    ffn_grad = dot_back(gug[own_rows, :], gu[...].reshape(640, 4096))
    hidden_grad = out_grad + norm_back(hidden, r_hidden, g_pre, ffn_grad)
    put_gain(4, gain_grad(hidden, r_hidden, ffn_grad))
    hidden_grad_s[...] = hidden_grad
    proj_grad = norm_back(proj, r_proj, g_post, hidden_grad).astype(BF)
    put_gain(3, gain_grad(proj, r_proj, hidden_grad))
    projg[own_rows, :] = proj_grad
    shared["projg"] = share(projg)
    def cols(start, width):
        return pl.ds(pl.multiple_of(start, 128), width)

    def put(g, off, n, value, col_blocks):
        value = value.astype(BF)
        for yq in range(4):
            for j in range(col_blocks):
                g[yq, pl.ds(off + j * n, n), :] = value[yq * n : yq * n + n, j * 128 : j * 128 + 128]

    for name in ("ffn", "gug"):
        shared[name].wait_recv()
    for part in range(2):
        put(ge, OFF_G + part * 640, 160, tdot(ffn[...], gug[:, cols(c * 1024 + part * 512, 512)]), 4)
        put(ge, OFF_U + part * 640, 160, tdot(ffn[...], gug[:, cols(2048 + c * 1024 + part * 512, 512)]), 4)
    early_a = Group(net, ge, e_full, EA_PARTS, group_b[0], relay=True)
    early_a.step()
    attn_grad = dot_back(proj_grad, w_out).astype(BF)
    for h in range(4):
        do_s[pl.ds(h * 128, 128), :] = attn_grad[:, h * 256 : h * 256 + 256]
    delta_s[...] = jnp.sum(do_s[...].astype(F32) * acc[...], axis=1, keepdims=True)

    for name in ("attn", "mixed", "downg", "projg"):
        shared[name].wait_recv()
    for yq in range(4):
        value = tdot(attn[:, cols(yq * 256 + c * 128, 128)], projg[...]).astype(BF)
        for j in range(5):
            ge[yq, pl.ds(OFF_O + j * 128, 128), :] = value[:, j * 128 : j * 128 + 128]
        value = tdot(mixed[:, cols(yq * 512 + c * 256, 256)], downg[...]).astype(BF)
        for j in range(5):
            ge[yq, pl.ds(OFF_D + j * 256, 256), :] = value[:, j * 128 : j * 128 + 128]
    early_b = Group(net, ge, e_full, EB_PARTS, group_b[1])
    early_b.step()

    acc[...] = jnp.zeros_like(acc)

    def tile(cc, j, diagonal):
        kt, vt = k_all[cc, j].reshape(512, 256), v_all[cc, j].reshape(512, 256)
        p = jnp.exp(dot_back(q_s[...], kt)) * inv_s[...]
        if diagonal:
            p = jnp.where(causal(net, cc), p, 0.0)
        ds = (p * (dot_back(do_s[...], vt) - delta_s[...])).astype(BF)
        acc[...] += dot(ds, kt)
        dk[cc, j] = tdot(ds, q_s[...]).astype(BF).reshape(4, 128, 256)
        dv[cc, j] = tdot(p.astype(BF), do_s[...]).astype(BF).reshape(4, 128, 256)

    kc, vc = {}, {}

    def tiles(s):
        j = net.at("z", s)

        def step(i, _):
            cc = lax.rem(other + i, 2)
            if s == 0:
                tile(cc, j, True)
            else:

                @pl.when(j < z)
                def _():
                    tile(cc, j, False)

                @pl.when(j > z)
                def _():
                    dk[cc, j] = jnp.zeros((4, 128, 256), BF)
                    dv[cc, j] = jnp.zeros((4, 128, 256), BF)

            return 0

        lax.fori_loop(0, 2, step, 0)
        kc[s] = net.copy(dk.at[other, j], kin.at[j], "c")
        vc[s] = net.copy(dv.at[other, j], vin.at[j], "c")

    k1 = Scatter(net, "z", lambda j: kin.at[j], kbufs)
    v1 = Scatter(net, "x", lambda j: vin.at[:, j], vbufs)
    k2 = Scatter(net, "x", lambda j: kin.at[z, j], k2bufs)
    v2 = Scatter(net, "z", lambda j: vin.at[j, x], v2bufs)

    def take(s):
        j = net.at("z", s)
        kc[s].wait_recv()
        add_rows(kin.at[j], (dk.at[c, j],))
        if s != 0:
            k1.send(s)
        vc[s].wait_recv()
        add_rows(vin.at[j], (dv.at[c, j],))

    tiles(2)
    tiles(1)
    take(2)
    tiles(-1)
    take(1)
    early_a.mid()
    tiles(0)
    take(-1)
    take(0)
    v1.start()

    total_q = jnp.zeros((1, 256), F32)
    for h in range(4):
        v = raw[:, pl.ds(h * 256, 256)]
        r = rms(v)
        u = rope_back(acc[pl.ds(h * 128, 128), :] * 0.0625, cos[...], sin[...])
        total_q += gain_grad(v, r, u)
        qkvg[own_rows, pl.ds(h * 256, 256)] = norm_back(v, r, g_q, u).astype(BF)
    put_gain(1, total_q)
    q_cols, kv_cols = pl.ds(0, 1024), pl.ds(1024, 512)
    share_q = net.copy(qkvg.at[own_rows, q_cols], qkvg.at[other_rows, q_cols], "c")
    normed_grad = dot_back(qkvg[own_rows, q_cols], qkv_all[:, :, q_cols].reshape(640, 1024))
    early_b.step()
    shared["normed"].wait_recv()
    share_q.wait_recv()
    put(gm, OFF_Q, 160, tdot(normed[...], qkvg[:, cols(c * 512, 512)]), 4)
    middle = Group(net, gm, m_full, M_PARTS, group_b[2])
    k1.end()
    k2.start()
    v1.end()
    v2.start()
    middle.step()
    early_b.step()
    early_a.step()
    k2.end()
    v2.end()

    v = raw[:, pl.ds(1024, 256)]
    r = rms(v)
    u = rope_back(kin[z, x].astype(F32), cos[...], sin[...])
    qkvg[own_rows, pl.ds(1024, 256)] = norm_back(v, r, g_k, u).astype(BF)
    qkvg[own_rows, pl.ds(1280, 256)] = vin[z, x]
    share_kv = net.copy(qkvg.at[own_rows, kv_cols], qkvg.at[other_rows, kv_cols], "c")
    put_gain(2, gain_grad(v, r, u))
    normed_grad = normed_grad + dot_back(qkvg[own_rows, kv_cols], qkv_all[:, :, kv_cols].reshape(640, 512))
    t = tokens[...].astype(F32)
    r = rms(t)
    put_gain(0, gain_grad(t, r, normed_grad))
    gain_copy = net.copy(gain_s, gain_other, "c")
    input_grad[...] = hidden_grad_s[...] + norm_back(t, r, g_in, normed_grad)
    share_kv.wait_recv()
    put(gl, OFF_K, 160, tdot(normed[...], qkvg[:, cols(1024 + c * 128, 128)]), 1)
    put(gl, OFF_V, 160, tdot(normed[...], qkvg[:, cols(1280 + c * 128, 128)]), 1)
    gain_copy.wait_recv()
    gl[:, pl.ds(OFF_GAIN, 16), :] = (gain_s[...] + gain_other[...]).astype(BF)
    late = Group(net, gl, l_full, L_PARTS, group_b[3])
    late.step()
    middle.step()
    early_a.step()
    early_b.step()
    middle.step()
    late.step()
    early_a.step()
    early_b.step()
    middle.step()
    late.step()
    early_a.step()
    early_b.step()
    middle.step()
    late.step()
    early_a.step()
    middle.step()
    late.step()
    early_a.step()
    late.step()
    early_b.step()
    e_copy = pltpu.make_async_copy(e_full, e_out, own_sem.at[0])
    e_copy.start()
    middle.step()
    m_copy = pltpu.make_async_copy(m_full, m_out, own_sem.at[1])
    m_copy.start()
    late.step()
    e_copy.wait()
    m_copy.wait()
    net.drain()


def layer(*args):
    def s(dtype, *shape):
        return jax.ShapeDtypeStruct(shape, dtype)

    n = 6 + 4 + 3 + 18 + 18 + 3 + 4 + 4 + 3 + 3 + 3 + 12 + 8 + 8 + 2 + 8 + 12 + sum(16 * len(p) + 1 for p in ALL_PARTS)
    big, small = VMEM((4, 128, 256), BF), VMEM((128, 256), BF)
    whole = VMEM((2, 4, 4, 128, 256), BF)
    column = VMEM((512, 1), F32)
    return pl.pallas_call(
        layer_kernel,
        out_shape=(
            s(BF, 128, 640), s(F32, 128, 640), s(BF, 2, E_ROWS, 128), s(BF, 2, M_ROWS, 128), s(BF, 2, L_ROWS, 128)
        ),
        in_specs=[ANYSPEC] * 7 + [VSPEC] * 6 + [ANYSPEC] * 2 + [VSPEC] * 2,
        out_specs=[VSPEC, VSPEC, ANYSPEC, ANYSPEC, VSPEC],
        scratch_shapes=[
            VMEM((2, E_ROWS, 128), BF), VMEM((2, M_ROWS, 128), BF),
            VMEM((4, 160, 1536), BF), VMEM((4, 160, 4096), BF), VMEM((4, 256, 640), BF), VMEM((4, 512, 640), BF),
            whole, whole,
            *[VMEM((256, n), BF) for n in (640, 1536, 1024, 640, 640, 4096, 2048, 640)],
            VMEM((4, 8, 256), F32), VMEM((8, 640), F32), VMEM((4, 16, 128), F32), VMEM((4, 16, 128), F32),
            VMEM((4, E_ROWS, 128), BF), VMEM((4, M_ROWS, 128), BF), VMEM((4, L_ROWS, 128), BF),
            VMEM((128, 128), F32), VMEM((128, 128), F32), VMEM((128, 640), BF), VMEM((128, 640), BF),
            whole, whole, VMEM((4, 4, 128, 256), BF), VMEM((4, 4, 128, 256), BF),
            VMEM((512, 256), F32), column, column, VMEM((512, 256), BF), VMEM((512, 256), BF), VMEM((128, 1280), F32),
            VMEM((128, 2048), F32), VMEM((128, 2048), F32), VMEM((128, 640), F32),
            *[big] * 6, *[small] * 6,
            *[b for parts in ALL_PARTS for b in group_bufs(parts)],
            pltpu.SemaphoreType.DMA((n,)),
            pltpu.SemaphoreType.DMA((n,)),
            pltpu.SemaphoreType.DMA((9,)),
        ],
        compiler_params=pltpu.CompilerParams(collective_id=0, has_side_effects=True, vmem_limit_bytes=VMEM_LIMIT),
        name="layer",
    )(*args)


def unpack_kernel(e, m, l, lo, ig, lo_out, ig_out, oq, ok, ov, oo, og, ou, od, *gain_outs):
    lo_out[...] = lo[...]
    ig_out[...] = ig[...]
    for c in range(2):

        def block(full, off, n, j):
            return full[c, pl.ds(off + j * n, n), :].astype(F32)

        for j in range(4):
            oq[:, pl.ds(c * 512 + j * 128, 128)] = block(m, OFF_Q, 160, j)
        ok[:, pl.ds(c * 128, 128)] = block(l, OFF_K, 160, 0)
        ov[:, pl.ds(c * 128, 128)] = block(l, OFF_V, 160, 0)
        for j in range(8):
            og[:, pl.ds(c * 1024 + j * 128, 128)] = block(e, OFF_G, 160, j)
            ou[:, pl.ds(c * 1024 + j * 128, 128)] = block(e, OFF_U, 160, j)
        for j in range(5):
            oo[pl.ds(c * 128, 128), pl.ds(j * 128, 128)] = block(e, OFF_O, 128, j)
            od[pl.ds(c * 256, 256), pl.ds(j * 128, 128)] = block(e, OFF_D, 256, j)
    rows = l[0, pl.ds(OFF_GAIN, 16), :].astype(F32)
    for i, n in enumerate(GAIN_SIZES):
        gain_outs[i][:, pl.ds(0, min(n, 128))] = rows[2 * i : 2 * i + 1, : min(n, 128)]
        if n > 128:
            gain_outs[i][:, pl.ds(128, n - 128)] = rows[2 * i + 1 : 2 * i + 2, : n - 128]


def unpack(e, m, l, lo, ig):
    def s(*shape):
        return jax.ShapeDtypeStruct(shape, F32)

    return pl.pallas_call(
        unpack_kernel,
        out_shape=(
            jax.ShapeDtypeStruct((128, 640), BF), s(128, 640), s(160, 1024), s(160, 256), s(160, 256), s(256, 640), s(160, 2048), s(160, 2048), s(512, 640),
            *[s(1, n) for n in GAIN_SIZES],
        ),
        in_specs=[VSPEC] * 5,
        out_specs=[VSPEC] * 15,
        compiler_params=pltpu.CompilerParams(vmem_limit_bytes=VMEM_LIMIT),
        name="unpack",
    )(e, m, l, lo, ig)


def local(
    tokens, positions, w_query, w_key, w_value, w_out, w_gate, w_up, w_down,
    gain_in, gain_query, gain_key, gain_attn_post, gain_ffn_pre, gain_ffn_post, cotangent,
):
    gains = (gain_in, gain_query, gain_key, gain_attn_post, gain_ffn_pre, gain_ffn_post)
    exponents = jnp.arange(0, 256, 2, dtype=F32) / 256
    inverse = 1.0 / ROPE_BASE**exponents
    layer_out, input_grad, e_full, m_full, l_full = layer(
        w_query, w_key, w_value, w_out, w_gate, w_up, w_down, *gains, tokens, cotangent, positions, inverse.reshape(1, 128)
    )
    layer_out, input_grad, oq, ok, ov, oo, og, ou, od, *gain_grads = unpack(e_full, m_full, l_full, layer_out, input_grad)
    return (layer_out, input_grad, oq, ok, ov, oo, og, ou, od, *[g.reshape(g.shape[1]) for g in gain_grads])


def solution(mesh):
    rows, both, vec = P("fsdp", None), P(("fsdp", "ctx"), None), P("fsdp")
    in_specs = (both, P(("fsdp", "ctx")), *[rows] * 7, *[vec] * 6, both)
    out_specs = (both, both, *[rows] * 7, *[vec] * 6)
    return jax.shard_map(local, mesh=mesh, in_specs=in_specs, out_specs=out_specs, check_vma=False)
```
